256 devices in a mesh: row: 16 (over y_hi, z), col: 16 (over y_lo, x, core).
Axes of the slice: x: 4, y: 4 (y_hi: 2, y_lo: 2; y = y_hi * 2 + y_lo), z: 8, core: 2. Of those that a mesh axis runs over, the one named last changes fastest.
Arguments:
- design: bfloat16 [256, 24576], P('row', 'col'), may hold values from -0.375 to 0.375
- filter_taps: float32 [256], replicated, may hold values from -0.21875 to 0.21875
- probes: float32 [24576, 128], P('row', 'col'), may hold values from -576 to 576
- lower_bound: float32 [1], replicated, may hold values from 6 to 24
- upper_bound: float32 [1], replicated, may hold values from 192 to 288
Outputs:
- normal: float32 [24576, 24576], P('row', 'col')
- solution: float32 [24576, 128], P('row', 'col')
The draws below stay inside these ranges and needn't reach their ends.
All inputs are finite; a program needn't handle non-finite values.
Results may differ from the reference program's by a relative error of at most 0.0072.
The reference program's roundings to bfloat16 on the way (of `filter_matrix` and `white`) count: a program that leaves them out, or rounds other values in their place, can miss the bound.
Values may be sent and summed in bfloat16 or wider, within the bound.
A program may use at most 64 MiB of HBM per device.

```python
import jax
import jax.numpy as jnp
from jax import lax

P_SIZE = 24576
EPOCHS = 256
NPROBE = 128
SWEEPS = 2


def level_of(rng, shape, pieces, low, high):
    factor_of, own = 1.0, jax.random.fold_in(rng, 6)
    for dim, blocks in pieces:
        steps = jnp.exp(jax.random.uniform(jax.random.fold_in(own, dim), (blocks,), jnp.float32, low / len(pieces), high / len(pieces)))
        factor_of = factor_of * jnp.repeat(steps, shape[dim] // blocks).reshape([-1 if axis == dim else 1 for axis in range(len(shape))])
    return factor_of


def gaussian(rng, extent, spread, reach, shards=(), held_as=jnp.bfloat16):
    array = spread * jax.random.normal(rng, extent, jnp.float32)
    if shards:
        array = array * level_of(rng, extent, shards, -0.22, 0.18)
    return jnp.clip(array, -reach, reach).astype(held_as)


def setup_inputs(seed: int = 0) -> dict:
    key_of = jax.random.split(jax.random.key(seed), 6)
    design = gaussian(key_of[0], (EPOCHS, P_SIZE), EPOCHS ** -0.5, 0.375, ((0, 16), (1, 16)))
    filter_taps = gaussian(key_of[1], (EPOCHS,), (3 * EPOCHS) ** -0.5, 0.21875, (), jnp.float32)
    probes = gaussian(key_of[2], (P_SIZE, NPROBE), (P_SIZE // EPOCHS), 576.0, ((0, 16), (1, 16)), jnp.float32)
    lower_bound = jnp.clip(jax.random.uniform(key_of[3], (1,), jnp.float32, 6.0, 24.0), 6.0, 24.0)
    upper_bound = jnp.clip(jax.random.uniform(key_of[4], (1,), jnp.float32, 192.0, 288.0), 192.0, 288.0)
    return {"design": design, "filter_taps": filter_taps, "probes": probes, "lower_bound": lower_bound, "upper_bound": upper_bound}


def whitening(filter_taps):
    count = filter_taps.shape[0]
    padded = jnp.concatenate([filter_taps, jnp.zeros_like(filter_taps)])
    repeated = jnp.tile(padded, count)[:count * (2 * count - 1)]
    upper = repeated.reshape(count, 2 * count - 1)[:, :count]
    matrix = upper.T + jnp.eye(count, dtype=filter_taps.dtype)
    return matrix.astype(jnp.bfloat16)


def reference(design, filter_taps, probes, lower_bound, upper_bound):
    filter_matrix = whitening(filter_taps)
    white = jnp.dot(filter_matrix, design, preferred_element_type=jnp.float32).astype(jnp.bfloat16)
    normal = lax.dot_general(white, white, (((0,), (0,)), ((), ())), preferred_element_type=jnp.float32)
    jacobi = (jnp.sum(jnp.square(white.astype(jnp.float32)), axis=0) + 1e-6)[:, None]
    center_value = (lower_bound[0] + upper_bound[0]) / 2.0
    half_width = (upper_bound[0] - lower_bound[0]) / 2.0
    sigma_value = center_value / half_width
    weight_now = 1.0 / sigma_value
    residual = probes
    direction = residual / jacobi / center_value
    solution = jnp.zeros_like(probes)
    for sweep_index in range(SWEEPS):
        solution = solution + direction
        residual = residual - jnp.dot(normal, direction, precision=lax.Precision.HIGHEST)
        weight_next = 1.0 / (2.0 * sigma_value - weight_now)
        direction = weight_next * weight_now * direction + (2.0 * weight_next / half_width) * (residual / jacobi)
        weight_now = weight_next
    solution = solution + direction
    return normal, solution
```

```python
import jax
import jax.numpy as jnp
from jax import lax
from jax.experimental import pallas as pl
from jax.experimental.pallas import tpu as pltpu
from jax.sharding import PartitionSpec as P

MESH = pl.DeviceIdType.MESH
F32 = jnp.float32
BF16 = jnp.bfloat16
EPOCHS = 256
SIDE = 16
BLOCK = 16
WIDTH = 1536
LANES = 128
CHUNKS = WIDTH // LANES


def owner_of(chunk):
    return (chunk // 3) * 4 + chunk % 3


def remote(src, dst, send, recv, device):
    return pltpu.make_async_remote_copy(
        src_ref=src, dst_ref=dst, send_sem=send, recv_sem=recv, device_id=device, device_id_type=MESH
    )


def split(value):
    high = value.astype(BF16)
    low = (value - high.astype(F32)).astype(BF16)
    return jnp.concatenate([high, low], axis=0)


def kernel(
    design, taps, probes, lower, upper,
    tile, answer,
    cbuf, rsub, wr, wc, usend, ubuf,
    c_send, c_recv, s_send, s_recv, g_send, g_fwd, g_recv, u_send, u_recv,
):
    r, c = lax.axis_index("row"), lax.axis_index("col")
    h, z = r // 8, r % 8
    l, x, k = c // 8, (c // 2) % 4, c % 2
    sibling = (r, c + 1 - 2 * k)
    z_next, z_prev = (h * 8 + (z + 1) % 8, c), (h * 8 + (z + 7) % 8, c)
    partner = ((1 - h) * 8 + z, c)
    is_owner = c % 4 != 3
    mine = (c // 4) * 3 + c % 4
    on_diagonal = r == c

    barrier = pltpu.get_barrier_semaphore()
    for o in range(1, SIDE):
        pl.semaphore_signal(barrier, inc=1, device_id=((r + o) % SIDE, c), device_id_type=MESH)
    for dl in range(2):
        for dx in range(4):
            if dl or dx:
                to = (r, ((l + dl) % 2) * 8 + ((x + dx) % 4) * 2 + k)
                pl.semaphore_signal(barrier, inc=1, device_id=to, device_id_type=MESH)
    pl.semaphore_signal(barrier, inc=1, device_id=sibling, device_id_type=MESH)
    for o in range(1, SIDE):
        pl.semaphore_signal(barrier, inc=1, device_id=((r + o) % SIDE, r), device_id_type=MESH)

    @pl.when(jnp.logical_not(on_diagonal))
    def _():
        pl.semaphore_signal(barrier, inc=1, device_id=(r, r), device_id_type=MESH)

    pl.semaphore_wait(barrier, 15 + 8 + 15 + jnp.where(on_diagonal, 0, 1))

    def block_of(other, steps):
        return ((1 - h) if other else h) * 8 + (z + steps + 16) % 8

    sends = []

    def ship(slot, block, to, src=None):
        copy = remote(
            cbuf.at[block] if src is None else src, cbuf.at[block], c_send.at[slot], c_recv.at[block], to
        )
        copy.start()
        sends.append(copy)

    def await_block(block):
        remote(cbuf.at[block], cbuf.at[block], c_send.at[0], c_recv.at[block], z_next).wait_recv()

    ship(0, r, z_next, design)
    ship(1, r, z_prev, design)
    ship(2, r, partner, design)

    scatter = []
    for chunk in range(CHUNKS):
        owner = owner_of(chunk)
        copy = remote(
            design.at[:, pl.ds(chunk * LANES, LANES)], rsub.at[r], s_send.at[chunk], s_recv.at[r], (c, owner)
        )
        away = jnp.logical_not(jnp.logical_and(on_diagonal, c == owner))
        scatter.append((away, copy))

        @pl.when(away)
        def _():
            copy.start()

        @pl.when(jnp.logical_not(away))
        def _():
            rsub[r] = design[:, chunk * LANES : (chunk + 1) * LANES]

    cbuf[r] = design[...]

    shape = (EPOCHS, EPOCHS)
    row_id = lax.broadcasted_iota(jnp.int32, shape, 0)
    col_id = lax.broadcasted_iota(jnp.int32, shape, 1)
    moved = jnp.broadcast_to(taps[...], shape)
    for bit in range(8):
        moved = jnp.where((row_id >> bit) % 2 == 1, pltpu.roll(moved, 1 << bit, 1), moved)
    moved = jnp.where(col_id >= row_id, moved, 0.0) + jnp.where(col_id == row_id, 1.0, 0.0)
    filt = moved.T.astype(BF16)

    def whiten(raw):
        return jnp.dot(filt, raw, preferred_element_type=F32).astype(BF16)

    await_block(block_of(False, -1))
    ship(3, block_of(False, -1), z_next)
    await_block(block_of(False, 1))
    ship(4, block_of(False, 1), z_prev)
    await_block(block_of(True, 0))
    ship(5, block_of(True, 0), z_next)
    ship(6, block_of(True, 0), z_prev)

    gather = []

    @pl.when(is_owner)
    def _():
        for o in range(SIDE):
            source = (r + o) % SIDE

            def arrived():
                remote(rsub.at[source], rsub.at[source], s_send.at[0], s_recv.at[source], z_next).wait_recv()

            if o == 0:
                pl.when(jnp.logical_not(on_diagonal))(arrived)
            else:
                arrived()
        wr[mine] = whiten(rsub[...].reshape(EPOCHS, LANES))
        slot = 0
        for dl in range(2):
            for dx in range(4):
                to = sibling
                if dl or dx:
                    to = (r, ((l + dl) % 2) * 8 + ((x + dx) % 4) * 2 + k)
                copy = remote(wr.at[mine], wr.at[mine], g_send.at[slot], g_recv.at[mine], to)
                copy.start()
                gather.append(copy)
                slot += 1

    await_block(block_of(False, -2))
    ship(7, block_of(False, -2), z_next)
    await_block(block_of(False, 2))
    ship(8, block_of(False, 2), z_prev)
    await_block(block_of(True, -1))
    ship(9, block_of(True, -1), z_next)
    await_block(block_of(True, 1))
    ship(10, block_of(True, 1), z_prev)

    await_block(block_of(False, -3))
    await_block(block_of(False, 3))
    way = 1 - 2 * h
    own_way = (h * 8 + (z + way + 8) % 8, c)
    other_way = (h * 8 + (z - way + 8) % 8, c)
    ship(11, block_of(False, -3 * way), own_way)
    await_block(block_of(True, -2))
    ship(12, block_of(True, -2), z_next)
    await_block(block_of(True, 2))
    ship(13, block_of(True, 2), z_prev)

    forwards = []

    def chunk_arrived(chunk):
        remote(wr.at[chunk], wr.at[chunk], g_fwd.at[chunk], g_recv.at[chunk], sibling).wait_recv()

    for chunk in range(CHUNKS):
        owner = owner_of(chunk)
        relay = jnp.logical_and(c != owner, k == owner % 2)
        copy = remote(wr.at[chunk], wr.at[chunk], g_fwd.at[chunk], g_recv.at[chunk], sibling)
        forwards.append((relay, copy))

        @pl.when(relay)
        def _():
            chunk_arrived(chunk)
            copy.start()

    await_block(block_of(True, -3))
    await_block(block_of(True, 3))
    ship(14, block_of(True, 3 * way), other_way)

    for chunk in range(CHUNKS):
        owner = owner_of(chunk)

        @pl.when(k != owner % 2)
        def _():
            chunk_arrived(chunk)

    low = jnp.full((1, LANES), lower[0], F32)
    high = jnp.full((1, LANES), upper[0], F32)
    center = (low + high) / 2.0
    half = (high - low) / 2.0
    sigma = center / half
    rho0 = 1.0 / sigma
    rho1 = 1.0 / (2.0 * sigma - rho0)
    rho2 = 1.0 / (2.0 * sigma - rho1)

    last = (((1,), (1,)), ((), ()))

    def forward_product(parts):
        total = jnp.zeros((2 * 8, EPOCHS), F32)
        for chunk in range(CHUNKS):
            total += lax.dot_general(split(parts[chunk]), wr[chunk], last, preferred_element_type=F32)
        return total[:8] + total[8:]

    def back_product(whole, chunk):
        both = jnp.dot(whole, wr[chunk], preferred_element_type=F32)
        return both[:8] + both[8:]

    pending = []

    def exchange_start(turn, value):
        packed = jnp.concatenate([value[:, :LANES], value[:, LANES:]], axis=0).astype(BF16)
        usend[turn] = packed
        ubuf[turn, r] = packed
        for o in range(1, SIDE):
            copy = remote(
                usend.at[turn], ubuf.at[turn, r], u_send.at[turn, o], u_recv.at[turn, r], ((r + o) % SIDE, c)
            )
            copy.start()
            pending.append(copy)

    def exchange_finish(turn):
        for o in range(1, SIDE):
            source = (r + o) % SIDE
            slot = ubuf.at[turn, source]
            remote(slot, slot, u_send.at[turn, o], u_recv.at[turn, source], z_next).wait_recv()
        total = jnp.sum(ubuf[turn].astype(F32), axis=0)
        return jnp.concatenate([total[:8], total[8:]], axis=1)

    def rows_of(first, count):
        @pl.loop(first, first + count)
        def _(chunk):
            tile[pl.ds(pl.multiple_of(chunk * LANES, LANES), LANES), :] = lax.dot_general(
                wr[chunk], wc[...], (((0,), (0,)), ((), ())), preferred_element_type=F32
            )

    inverse, residual, direction = [], [], []
    for chunk in range(CHUNKS):
        wide = wr[chunk].astype(F32)
        jacobi = jnp.sum(wide * wide, axis=0, keepdims=True) + 1e-06
        right = probes[:, chunk * LANES : (chunk + 1) * LANES]
        inverse.append(1.0 / jacobi)
        residual.append(right)
        direction.append(right / jacobi / center)
    total = list(direction)
    exchange_start(0, forward_product(direction))

    await_block(block_of(False, 4))
    await_block(block_of(True, 4))
    wc[...] = whiten(cbuf[...].reshape(EPOCHS, WIDTH))
    rows_of(0, 6)

    product = split(exchange_finish(0))
    for chunk in range(CHUNKS):
        residual[chunk] = residual[chunk] - back_product(product, chunk)
        direction[chunk] = rho1 * rho0 * direction[chunk] + 2.0 * rho1 / half * (
            residual[chunk] * inverse[chunk]
        )
        total[chunk] = total[chunk] + direction[chunk]
    exchange_start(1, forward_product(direction))
    rows_of(6, 6)
    product = split(exchange_finish(1))
    for chunk in range(CHUNKS):
        residual[chunk] = residual[chunk] - back_product(product, chunk)
        direction[chunk] = rho2 * rho1 * direction[chunk] + 2.0 * rho2 / half * (
            residual[chunk] * inverse[chunk]
        )
        answer[:, chunk * LANES : (chunk + 1) * LANES] = total[chunk] + direction[chunk]

    for copy in sends + pending:
        copy.wait_send()
    for away, copy in scatter + forwards:
        pl.when(away)(copy.wait_send)

    @pl.when(is_owner)
    def _():
        for slot in range(8):
            remote(wr.at[mine], wr.at[mine], g_send.at[slot], g_recv.at[mine], sibling).wait_send()


def body(design, filter_taps, probes, lower_bound, upper_bound):
    vmem = pl.BlockSpec(memory_space=pltpu.VMEM)
    smem = pl.BlockSpec(memory_space=pltpu.SMEM)
    dma = pltpu.SemaphoreType.DMA
    tile, answer = pl.pallas_call(
        kernel,
        out_shape=(
            jax.ShapeDtypeStruct((WIDTH, WIDTH), F32),
            jax.ShapeDtypeStruct((8, WIDTH), F32),
        ),
        in_specs=[vmem, vmem, vmem, smem, smem],
        out_specs=(vmem, vmem),
        scratch_shapes=[
            pltpu.VMEM((SIDE, BLOCK, WIDTH), BF16),
            pltpu.VMEM((SIDE, BLOCK, LANES), BF16),
            pltpu.VMEM((CHUNKS, EPOCHS, LANES), BF16),
            pltpu.VMEM((EPOCHS, WIDTH), BF16),
            pltpu.VMEM((2, 16, LANES), BF16),
            pltpu.VMEM((2, SIDE, 16, LANES), BF16),
            dma((15,)), dma((SIDE,)),
            dma((CHUNKS,)), dma((SIDE,)),
            dma((8,)), dma((CHUNKS,)), dma((CHUNKS,)),
            dma((2, SIDE)), dma((2, SIDE)),
        ],
        compiler_params=pltpu.CompilerParams(
            collective_id=1, has_side_effects=True, vmem_limit_bytes=40 << 20
        ),
        name="gather_and_solve",
    )(design, filter_taps.reshape(1, EPOCHS), probes.T, lower_bound, upper_bound)
    return tile, answer.T


def solution(mesh):
    placed = (P("row", "col"), P(), P("row", "col"), P(), P())
    return jax.shard_map(
        body,
        mesh=mesh,
        in_specs=placed,
        out_specs=(P("row", "col"), P("row", "col")),
        check_vma=False,
    )
```

```python
import jax
import jax.numpy as jnp
from jax import lax
from jax.experimental import pallas as pl
from jax.experimental.pallas import tpu as pltpu
from jax.sharding import PartitionSpec as P

MESH = pl.DeviceIdType.MESH
F32 = jnp.float32
BF16 = jnp.bfloat16
EPOCHS = 256
SIDE = 16
BLOCK = 16
WIDTH = 1536
LANES = 128
CHUNKS = WIDTH // LANES
STEP = 256
STEPS = WIDTH // STEP
GRANT = 54 << 20
FIRST = (((0,), (0,)), ((), ()))
LAST = (((1,), (1,)), ((), ()))


def owner_of(chunk):
    return (chunk // 3) * 4 + chunk % 3


def remote(src, dst, send, recv, device):
    return pltpu.make_async_remote_copy(
        src_ref=src, dst_ref=dst, send_sem=send, recv_sem=recv, device_id=device, device_id_type=MESH
    )


def split(value):
    high = value.astype(BF16)
    low = (value - high.astype(F32)).astype(BF16)
    return jnp.concatenate([high, low], axis=0)


def pair_sum(value):
    rows = value.shape[0] // 2
    return value[:rows] + value[rows:]


def squares_over_epochs(transposed):
    wide = transposed.astype(F32)
    parts = split(wide * wide)
    rows = transposed.shape[0]
    ones = jnp.ones((8, EPOCHS), BF16)
    both = lax.dot_general(ones, parts, LAST, preferred_element_type=F32)
    return both[:, :rows] + both[:, rows:] + 1e-06


def pack(value):
    return jnp.concatenate([value[:, :LANES], value[:, LANES:]], axis=0).astype(BF16)


def kernel(
    design_in, taps_in, probes_in, lower, upper,
    rt_out, c_out, answer_out,
    answer, design, taps, probes,
    cbuf, rsub, psub, filt, filt_t, white_rt, white_c, usend, ubuf, rs_send, rs_buf,
    in_sem, out_sem, c_send, c_recv, s_send, s_recv, p_send, p_recv, rs_ssem, rs_rsem,
    g_send, g_fwd, g_recv, u_send, u_recv,
):
    r, c = lax.axis_index("row"), lax.axis_index("col")
    h, z = r // 8, r % 8
    l, x, k = c // 8, (c // 2) % 4, c % 2
    sibling = (r, c + 1 - 2 * k)
    z_next, z_prev = (h * 8 + (z + 1) % 8, c), (h * 8 + (z + 7) % 8, c)
    partner = ((1 - h) * 8 + z, c)
    is_owner = c % 4 != 3
    mine = (c // 4) * 3 + c % 4
    on_diagonal = r == c

    loads = [
        pltpu.make_async_copy(src, dst, in_sem.at[i])
        for i, (src, dst) in enumerate(((design_in, design), (taps_in, taps), (probes_in, probes)))
    ]
    for load in loads:
        load.start()

    barrier = pltpu.get_barrier_semaphore()
    for o in range(1, SIDE):
        pl.semaphore_signal(barrier, inc=1, device_id=((r + o) % SIDE, r), device_id_type=MESH)

    @pl.when(jnp.logical_not(on_diagonal))
    def _():
        pl.semaphore_signal(barrier, inc=1, device_id=(r, r), device_id_type=MESH)

    for o in range(1, SIDE):
        pl.semaphore_signal(barrier, inc=1, device_id=((r + o) % SIDE, c), device_id_type=MESH)
    for o in range(1, SIDE):
        pl.semaphore_signal(barrier, inc=1, device_id=(r, (c + o) % SIDE), device_id_type=MESH)

    loads[1].wait()
    shape = (EPOCHS, EPOCHS)
    row_id = lax.broadcasted_iota(jnp.int32, shape, 0)
    col_id = lax.broadcasted_iota(jnp.int32, shape, 1)
    moved = jnp.broadcast_to(taps[...], shape)
    for bit in range(8):
        moved = jnp.where((row_id >> bit) % 2 == 1, pltpu.roll(moved, 1 << bit, 1), moved)
    moved = jnp.where(col_id >= row_id, moved, 0.0) + jnp.where(col_id == row_id, 1.0, 0.0)
    filt_t[...] = moved.astype(BF16)
    filt[...] = moved.T.astype(BF16)

    low = jnp.full((1, LANES), lower[0], F32)
    high = jnp.full((1, LANES), upper[0], F32)
    center = (low + high) / 2.0
    half = (high - low) / 2.0
    sigma = center / half
    rho0 = 1.0 / sigma
    rho1 = 1.0 / (2.0 * sigma - rho0)
    rho2 = 1.0 / (2.0 * sigma - rho1)

    def wide_row(row):
        return jnp.concatenate([row] * CHUNKS, axis=1)

    loads[0].wait()
    loads[2].wait()
    pl.semaphore_wait(barrier, 15 + 15 + 15 + jnp.where(on_diagonal, 0, 1))

    scatter = []
    for chunk in range(CHUNKS):
        owner = owner_of(chunk)
        copy = remote(
            design.at[:, pl.ds(chunk * LANES, LANES)], rsub.at[r], s_send.at[chunk], s_recv.at[r], (c, owner)
        )
        away = jnp.logical_not(jnp.logical_and(on_diagonal, c == owner))
        scatter.append((away, copy))

        @pl.when(away)
        def _():
            copy.start()

        @pl.when(jnp.logical_not(away))
        def _():
            rsub[r] = design[:, chunk * LANES : (chunk + 1) * LANES]

    def block_of(other, steps):
        return ((1 - h) if other else h) * 8 + (z + steps + 16) % 8

    sends = []

    def ship(slot, block, to, src=None):
        copy = remote(
            cbuf.at[block] if src is None else src, cbuf.at[block], c_send.at[slot], c_recv.at[block], to
        )
        copy.start()
        sends.append(copy)

    def await_block(block):
        remote(cbuf.at[block], cbuf.at[block], c_send.at[0], c_recv.at[block], z_next).wait_recv()

    way = 1 - 2 * h

    def at(steps):
        return (h * 8 + (z + steps + 8) % 8, c)

    ship(0, r, at(1), design)
    ship(1, r, at(-1), design)
    ship(2, r, partner, design)
    ship(3, r, at(2), design)
    ship(4, r, at(-2), design)
    for chunk in range(CHUNKS):
        owner = owner_of(chunk)
        copy = remote(
            probes.at[:, pl.ds(chunk * LANES, LANES)], psub.at[c], p_send.at[chunk], p_recv.at[c], (r, owner)
        )
        away = c != owner
        scatter.append((away, copy))

        @pl.when(away)
        def _():
            copy.start()

        @pl.when(jnp.logical_not(away))
        def _():
            psub[c] = probes[:, chunk * LANES : (chunk + 1) * LANES]

    cbuf[r] = design[...]

    await_block(block_of(True, 0))
    ship(5, block_of(True, 0), at(1))
    ship(6, block_of(True, 0), at(-1))
    ship(7, block_of(True, 0), at(2))
    ship(8, block_of(True, 0), at(-2))
    my_rows = pl.ds(pl.multiple_of(mine * LANES, LANES), LANES)

    @pl.when(is_owner)
    def _():
        for o in range(SIDE):
            source = (r + o) % SIDE

            def arrived():
                remote(rsub.at[source], rsub.at[source], s_send.at[0], s_recv.at[source], z_next).wait_recv()

            if o == 0:
                pl.when(jnp.logical_not(on_diagonal))(arrived)
            else:
                arrived()
        chunk_t = lax.dot_general(
            rsub[...].reshape(EPOCHS, LANES), filt_t[...], FIRST, preferred_element_type=F32
        ).astype(BF16)
        white_rt[my_rows, :] = chunk_t
        jacobi = squares_over_epochs(chunk_t)[:1]
        for o in range(1, SIDE):
            source = (c + o) % SIDE
            remote(psub.at[source], psub.at[source], p_send.at[0], p_recv.at[source], z_next).wait_recv()
        start = psub[...].reshape(SIDE * 8, LANES) / jacobi / center
        part = pair_sum(jnp.dot(split(start), chunk_t, preferred_element_type=F32))
        left = part[:, :LANES].reshape(SIDE, 8, LANES)
        right = part[:, LANES:].reshape(SIDE, 8, LANES)
        rs_send[...] = jnp.concatenate([left, right], axis=1).astype(BF16)
        for o in range(1, SIDE):
            to = (c + o) % SIDE
            remote(rs_send.at[to], rs_buf.at[mine], rs_ssem.at[o], rs_rsem.at[mine], (r, to)).start()
        rs_buf[mine] = rs_send[c]

    @pl.when(is_owner)
    def _():
        slot = 0
        for dl in range(2):
            for dx in range(4):
                to = sibling
                if dl or dx:
                    to = (r, ((l + dl) % 2) * 8 + ((x + dx) % 4) * 2 + k)
                remote(white_rt.at[my_rows], white_rt.at[my_rows], g_send.at[slot], g_recv.at[mine], to).start()
                slot += 1

    await_block(block_of(False, -2))
    ship(9, block_of(False, -2), at(1))
    await_block(block_of(False, 2))
    ship(10, block_of(False, 2), at(-1))
    ship(11, block_of(False, -2 * way), at(2 * way))
    await_block(block_of(True, -2))
    ship(12, block_of(True, -2), at(1))
    await_block(block_of(True, 2))
    ship(13, block_of(True, 2), at(-1))
    ship(14, block_of(True, 2 * way), at(-2 * way))
    def exchange_start(turn, packed):
        usend[turn] = packed
        ubuf[turn, r] = packed
        for o in range(1, SIDE):
            remote(
                usend.at[turn], ubuf.at[turn, r], u_send.at[turn, o], u_recv.at[turn, r], ((r + o) % SIDE, c)
            ).start()

    def exchange_finish(turn):
        for o in range(1, SIDE):
            source = (r + o) % SIDE
            slot = ubuf.at[turn, source]
            remote(slot, slot, u_send.at[turn, o], u_recv.at[turn, source], z_next).wait_recv()
        total = jnp.sum(ubuf[turn].astype(F32), axis=0)
        return split(jnp.concatenate([total[:8], total[8:]], axis=1))

    for chunk in range(CHUNKS):
        @pl.when(c != owner_of(chunk))
        def _():
            remote(
                rs_buf.at[chunk], rs_buf.at[chunk], rs_ssem.at[0], rs_rsem.at[chunk], sibling
            ).wait_recv()
    exchange_start(0, jnp.sum(rs_buf[...].astype(F32), axis=0).astype(BF16))

    forwards = []

    def chunk_copy(chunk):
        rows = white_rt.at[pl.ds(chunk * LANES, LANES)]
        return remote(rows, rows, g_fwd.at[chunk], g_recv.at[chunk], sibling)

    for chunk in range(CHUNKS):
        owner = owner_of(chunk)
        relay = jnp.logical_and(c != owner, k == owner % 2)
        copy = chunk_copy(chunk)
        forwards.append((relay, copy))

        @pl.when(relay)
        def _():
            copy.wait_recv()
            copy.start()

    for chunk in range(CHUNKS):
        @pl.when(k != owner_of(chunk) % 2)
        def _():
            chunk_copy(chunk).wait_recv()

    def back_product(whole):
        return pair_sum(lax.dot_general(whole, white_rt[...], LAST, preferred_element_type=F32))

    leave_rt = pltpu.make_async_copy(white_rt, rt_out, out_sem.at[0])
    leave_rt.start()
    jacobi = squares_over_epochs(white_rt[...])
    direction0 = probes[...] / jacobi / wide_row(center)
    residual1 = probes[...] - back_product(exchange_finish(0))
    direction1 = wide_row(rho1 * rho0) * direction0 + wide_row(2.0 * rho1 / half) * (residual1 / jacobi)
    exchange_start(
        1, pack(pair_sum(jnp.dot(split(direction1), white_rt[...], preferred_element_type=F32)))
    )

    for other in (False, True):
        for steps in (-3, -1, 1, 3, 4):
            await_block(block_of(other, steps))
    white_c[...] = jnp.dot(
        filt[...], cbuf[...].reshape(EPOCHS, WIDTH), preferred_element_type=F32
    ).astype(BF16)

    leave_c = pltpu.make_async_copy(white_c, c_out, out_sem.at[1])
    leave_c.start()

    residual2 = residual1 - back_product(exchange_finish(1))
    direction2 = wide_row(rho2 * rho1) * direction1 + wide_row(2.0 * rho2 / half) * (residual2 / jacobi)
    answer[...] = direction0 + direction1 + direction2
    leave_answer = pltpu.make_async_copy(answer, answer_out, out_sem.at[2])
    leave_answer.start()

    for copy in sends:
        copy.wait_send()
    for away, copy in scatter + forwards:
        pl.when(away)(copy.wait_send)
    for turn in range(2):
        for o in range(1, SIDE):
            remote(
                usend.at[turn], ubuf.at[turn, r], u_send.at[turn, o], u_recv.at[turn, r], z_next
            ).wait_send()

    @pl.when(is_owner)
    def _():
        for o in range(1, SIDE):
            remote(rs_send.at[0], rs_buf.at[mine], rs_ssem.at[o], rs_rsem.at[mine], z_next).wait_send()
        for slot in range(8):
            remote(white_rt.at[my_rows], white_rt.at[my_rows], g_send.at[slot], g_recv.at[mine], sibling).wait_send()

    leave_rt.wait()
    leave_c.wait()
    leave_answer.wait()


def tile_kernel(rt_in, c_in, answer_in, tile_out, answer_out, white_rt, white_c, answer, rows, in_sem, out_sem):
    load_c = pltpu.make_async_copy(c_in, white_c, in_sem.at[0])
    load_c.start()
    loads, leaves = [], []
    for part in range(STEPS):
        here = pl.ds(part * STEP, STEP)
        loads.append(pltpu.make_async_copy(rt_in.at[here], white_rt.at[here], in_sem.at[2 + part]))
        leaves.append(pltpu.make_async_copy(rows.at[part], tile_out.at[here], out_sem.at[1 + part]))
        loads[part].start()
    load_answer = pltpu.make_async_copy(answer_in, answer, in_sem.at[1])
    load_answer.start()
    load_c.wait()
    for part in range(STEPS):
        loads[part].wait()
        rows[part] = jnp.dot(
            white_rt[part * STEP : (part + 1) * STEP], white_c[...], preferred_element_type=F32
        )
        leaves[part].start()
    load_answer.wait()
    leave_answer = pltpu.make_async_copy(answer, answer_out, out_sem.at[0])
    leave_answer.start()
    for leave in leaves:
        leave.wait()
    leave_answer.wait()


def body(design, filter_taps, probes, lower_bound, upper_bound):
    smem = pl.BlockSpec(memory_space=pltpu.SMEM)
    hbm = pl.BlockSpec(memory_space=pltpu.HBM)
    dma = pltpu.SemaphoreType.DMA
    white_rt, white_c, answer = pl.pallas_call(
        kernel,
        out_shape=(
            jax.ShapeDtypeStruct((WIDTH, EPOCHS), BF16),
            jax.ShapeDtypeStruct((EPOCHS, WIDTH), BF16),
            jax.ShapeDtypeStruct((8, WIDTH), F32),
        ),
        in_specs=[hbm, hbm, hbm, smem, smem],
        out_specs=(hbm, hbm, hbm),
        scratch_shapes=[
            pltpu.VMEM((8, WIDTH), F32),
            pltpu.VMEM((BLOCK, WIDTH), BF16),
            pltpu.VMEM((1, EPOCHS), F32),
            pltpu.VMEM((8, WIDTH), F32),
            pltpu.VMEM((SIDE, BLOCK, WIDTH), BF16),
            pltpu.VMEM((SIDE, BLOCK, LANES), BF16),
            pltpu.VMEM((SIDE, 8, LANES), F32),
            pltpu.VMEM((EPOCHS, EPOCHS), BF16),
            pltpu.VMEM((EPOCHS, EPOCHS), BF16),
            pltpu.VMEM((WIDTH, EPOCHS), BF16),
            pltpu.VMEM((EPOCHS, WIDTH), BF16),
            pltpu.VMEM((2, 16, LANES), BF16),
            pltpu.VMEM((2, SIDE, 16, LANES), BF16),
            pltpu.VMEM((SIDE, 16, LANES), BF16),
            pltpu.VMEM((CHUNKS, 16, LANES), BF16),
            dma((3,)), dma((3,)),
            dma((15,)), dma((SIDE,)),
            dma((CHUNKS,)), dma((SIDE,)),
            dma((CHUNKS,)), dma((SIDE,)),
            dma((SIDE,)), dma((CHUNKS,)),
            dma((8,)), dma((CHUNKS,)), dma((CHUNKS,)),
            dma((2, SIDE)), dma((2, SIDE)),
        ],
        compiler_params=pltpu.CompilerParams(
            collective_id=1, has_side_effects=True, vmem_limit_bytes=GRANT
        ),
        name="gather_and_solve",
    )(design, filter_taps.reshape(1, EPOCHS), probes.T, lower_bound, upper_bound)
    tile, answer = pl.pallas_call(
        tile_kernel,
        out_shape=(
            jax.ShapeDtypeStruct((WIDTH, WIDTH), F32),
            jax.ShapeDtypeStruct((8, WIDTH), F32),
        ),
        in_specs=[hbm, hbm, hbm],
        out_specs=(hbm, hbm),
        scratch_shapes=[
            pltpu.VMEM((WIDTH, EPOCHS), BF16),
            pltpu.VMEM((EPOCHS, WIDTH), BF16),
            pltpu.VMEM((8, WIDTH), F32),
            pltpu.VMEM((STEPS, STEP, WIDTH), F32),
            dma((2 + STEPS,)), dma((1 + STEPS,)),
        ],
        compiler_params=pltpu.CompilerParams(vmem_limit_bytes=GRANT),
        name="normal_tile",
    )(white_rt, white_c, answer)
    return tile, answer.T


def solution(mesh):
    placed = (P("row", "col"), P(), P("row", "col"), P(), P())
    return jax.shard_map(
        body,
        mesh=mesh,
        in_specs=placed,
        out_specs=(P("row", "col"), P("row", "col")),
        check_vma=False,
    )
```

```python
import jax
import jax.numpy as jnp
from jax import lax
from jax.experimental import pallas as pl
from jax.experimental.pallas import tpu as pltpu
from jax.sharding import PartitionSpec as P

MESH = pl.DeviceIdType.MESH
F32 = jnp.float32
BF16 = jnp.bfloat16
EPOCHS = 256
SIDE = 16
BLOCK = 16
WIDTH = 1536
LANES = 128
CHUNKS = WIDTH // LANES
STEP = 256
STEPS = WIDTH // STEP
GRANT = 54 << 20
FIRST = (((0,), (0,)), ((), ()))
LAST = (((1,), (1,)), ((), ()))


def owner_of(chunk):
    return (chunk // 3) * 4 + chunk % 3


PLANE = tuple(sorted(((a, b) for a in range(2) for b in range(8) if a or b), key=lambda p: -(2 * p[0] + min(p[1], 8 - p[1]))))
ROW = tuple(
    sorted(
        ((a, b, d) for a in range(2) for b in range(4) for d in range(2) if a or b or d),
        key=lambda p: -(2 * (p[0] + min(p[1], 4 - p[1])) + p[2]),
    )
)


def remote(src, dst, send, recv, device):
    return pltpu.make_async_remote_copy(
        src_ref=src, dst_ref=dst, send_sem=send, recv_sem=recv, device_id=device, device_id_type=MESH
    )


def split(value):
    high = value.astype(BF16)
    low = (value - high.astype(F32)).astype(BF16)
    return jnp.concatenate([high, low], axis=0)


def pair_sum(value):
    rows = value.shape[0] // 2
    return value[:rows] + value[rows:]


def squares_over_epochs(transposed):
    wide = transposed.astype(F32)
    parts = split(wide * wide)
    rows = transposed.shape[0]
    ones = jnp.ones((8, EPOCHS), BF16)
    both = lax.dot_general(ones, parts, LAST, preferred_element_type=F32)
    return both[:, :rows] + both[:, rows:] + 1e-06


def pack(value):
    return jnp.concatenate([value[:, :LANES], value[:, LANES:]], axis=0).astype(BF16)


def back_product(whole, transposed):
    return pair_sum(lax.dot_general(whole, transposed, LAST, preferred_element_type=F32))


def kernel(
    design_in, taps_in, probes_in, lower, upper,
    rt_out, c_out, state_out, last_out,
    state, last, design, taps, probes,
    cbuf, rsub, psub, filt, filt_t, white_rt, white_c, usend, ubuf, rs_send, rs_buf,
    in_sem, out_sem, c_send, c_recv, s_send, s_recv, p_send, p_recv, rs_ssem, rs_rsem,
    g_send, g_fwd, g_recv, u_send, u_recv,
):
    r, c = lax.axis_index("row"), lax.axis_index("col")
    h, z = r // 8, r % 8
    l, x, k = c // 8, (c // 2) % 4, c % 2
    sibling = (r, c + 1 - 2 * k)
    z_next, z_prev = (h * 8 + (z + 1) % 8, c), (h * 8 + (z + 7) % 8, c)
    partner = ((1 - h) * 8 + z, c)
    is_owner = c % 4 != 3
    mine = (c // 4) * 3 + c % 4
    on_diagonal = r == c

    def in_plane(place):
        return ((h + place[0]) % 2) * 8 + (z + place[1]) % 8

    def in_row(place):
        return ((l + place[0]) % 2) * 8 + ((x + place[1]) % 4) * 2 + (k + place[2]) % 2

    loads = [
        pltpu.make_async_copy(src, dst, in_sem.at[i])
        for i, (src, dst) in enumerate(((design_in, design), (taps_in, taps), (probes_in, probes)))
    ]
    for load in loads:
        load.start()

    barrier = pltpu.get_barrier_semaphore()
    for o in range(1, SIDE):
        pl.semaphore_signal(barrier, inc=1, device_id=((r + o) % SIDE, r), device_id_type=MESH)

    @pl.when(jnp.logical_not(on_diagonal))
    def _():
        pl.semaphore_signal(barrier, inc=1, device_id=(r, r), device_id_type=MESH)

    for place in PLANE:
        pl.semaphore_signal(barrier, inc=1, device_id=(in_plane(place), c), device_id_type=MESH)
    for place in ROW:
        pl.semaphore_signal(barrier, inc=1, device_id=(r, in_row(place)), device_id_type=MESH)

    loads[1].wait()
    shape = (EPOCHS, EPOCHS)
    row_id = lax.broadcasted_iota(jnp.int32, shape, 0)
    col_id = lax.broadcasted_iota(jnp.int32, shape, 1)
    moved = jnp.broadcast_to(taps[...], shape)
    for bit in range(8):
        moved = jnp.where((row_id >> bit) % 2 == 1, pltpu.roll(moved, 1 << bit, 1), moved)
    moved = jnp.where(col_id >= row_id, moved, 0.0) + jnp.where(col_id == row_id, 1.0, 0.0)
    filt_t[...] = moved.astype(BF16)
    filt[...] = moved.T.astype(BF16)

    low = jnp.full((1, LANES), lower[0], F32)
    high = jnp.full((1, LANES), upper[0], F32)
    center = (low + high) / 2.0
    half = (high - low) / 2.0
    sigma = center / half
    rho0 = 1.0 / sigma
    rho1 = 1.0 / (2.0 * sigma - rho0)
    rho2 = 1.0 / (2.0 * sigma - rho1)

    def await_bytes(ref, sem):
        pltpu.make_async_copy(ref, ref, sem).wait()

    def wide_row(row):
        return jnp.concatenate([row] * CHUNKS, axis=1)

    loads[0].wait()
    loads[2].wait()
    pl.semaphore_wait(barrier, 15 + 15 + 15 + jnp.where(on_diagonal, 0, 1))

    for chunk in range(CHUNKS):
        owner = owner_of(chunk)
        copy = remote(
            design.at[:, pl.ds(chunk * LANES, LANES)], rsub.at[r], s_send, s_recv, (c, owner)
        )
        away = jnp.logical_not(jnp.logical_and(on_diagonal, c == owner))

        @pl.when(away)
        def _():
            copy.start()

        @pl.when(jnp.logical_not(away))
        def _():
            rsub[r] = design[:, chunk * LANES : (chunk + 1) * LANES]

    def block_of(other, steps):
        return ((1 - h) if other else h) * 8 + (z + steps + 16) % 8

    sends = []

    def ship(slot, block, to, src=None):
        copy = remote(
            cbuf.at[block] if src is None else src, cbuf.at[block], c_send.at[slot], c_recv.at[block], to
        )
        copy.start()
        sends.append(copy)

    def await_block(block):
        remote(cbuf.at[block], cbuf.at[block], c_send.at[0], c_recv.at[block], z_next).wait_recv()

    way = 1 - 2 * h

    def at(steps):
        return (h * 8 + (z + steps + 8) % 8, c)

    ship(0, r, at(1), design)
    ship(1, r, at(-1), design)
    ship(2, r, partner, design)
    ship(3, r, at(2), design)
    ship(4, r, at(-2), design)
    for chunk in range(CHUNKS):
        owner = owner_of(chunk)
        copy = remote(
            probes.at[:, pl.ds(chunk * LANES, LANES)], psub.at[c], p_send, p_recv, (r, owner)
        )
        away = c != owner

        @pl.when(away)
        def _():
            copy.start()

        @pl.when(jnp.logical_not(away))
        def _():
            psub[c] = probes[:, chunk * LANES : (chunk + 1) * LANES]

    cbuf[r] = design[...]

    await_block(block_of(True, 0))
    ship(5, block_of(True, 0), at(1))
    ship(6, block_of(True, 0), at(-1))
    ship(7, block_of(True, 0), at(2))
    ship(8, block_of(True, 0), at(-2))
    my_rows = pl.ds(pl.multiple_of(mine * LANES, LANES), LANES)

    @pl.when(is_owner)
    def _():
        await_bytes(psub.at[pl.ds(0, SIDE - 1)], p_recv)
        right = psub[...].reshape(SIDE * 8, LANES) / center

        @pl.when(on_diagonal)
        def _():
            await_bytes(rsub.at[pl.ds(0, SIDE - 1)], s_recv)

        @pl.when(jnp.logical_not(on_diagonal))
        def _():
            await_bytes(rsub, s_recv)

        raw = rsub[...].reshape(EPOCHS, LANES)
        chunk_t = lax.dot_general(raw, filt_t[...], FIRST, preferred_element_type=F32).astype(BF16)
        wide = jnp.dot(filt[...], raw, preferred_element_type=F32).astype(BF16).astype(F32)
        jacobi = jnp.sum(wide * wide, axis=0, keepdims=True) + 1e-06
        part = pair_sum(jnp.dot(split(right / jacobi), chunk_t, preferred_element_type=F32))
        left = part[:, :LANES].reshape(SIDE, 8, LANES)
        right = part[:, LANES:].reshape(SIDE, 8, LANES)
        rs_send[...] = jnp.concatenate([left, right], axis=1).astype(BF16)
        for place in ROW:
            to = in_row(place)
            remote(rs_send.at[to], rs_buf.at[mine], rs_ssem, rs_rsem, (r, to)).start()
        rs_buf[mine] = rs_send[c]
        white_rt[my_rows, :] = chunk_t
        for place in ROW:
            if not place[2]:
                remote(
                    white_rt.at[my_rows], white_rt.at[my_rows], g_send, g_recv.at[mine], (r, in_row(place))
                ).start()
        remote(white_rt.at[my_rows], white_rt.at[my_rows], g_send, g_recv.at[mine], sibling).start()

    await_block(block_of(False, -2))
    ship(9, block_of(False, -2), at(1))
    await_block(block_of(False, 2))
    ship(10, block_of(False, 2), at(-1))
    ship(11, block_of(False, -2 * way), at(2 * way))
    await_block(block_of(True, -2))
    ship(12, block_of(True, -2), at(1))
    await_block(block_of(True, 2))
    ship(13, block_of(True, 2), at(-1))
    ship(14, block_of(True, 2 * way), at(-2 * way))
    def exchange_start(turn, packed):
        usend[turn] = packed
        ubuf[turn, r] = packed
        for place in PLANE:
            remote(
                usend.at[turn], ubuf.at[turn, r], u_send.at[turn], u_recv.at[turn], (in_plane(place), c)
            ).start()

    def exchange_finish(turn):
        await_bytes(ubuf.at[turn, pl.ds(0, SIDE - 1)], u_recv.at[turn])
        total = jnp.sum(ubuf[turn].astype(F32), axis=0)
        return split(jnp.concatenate([total[:8], total[8:]], axis=1))

    @pl.when(is_owner)
    def _():
        await_bytes(rs_buf.at[pl.ds(0, CHUNKS - 1)], rs_rsem)

    @pl.when(jnp.logical_not(is_owner))
    def _():
        await_bytes(rs_buf, rs_rsem)

    exchange_start(0, jnp.sum(rs_buf[...].astype(F32), axis=0).astype(BF16))

    forwards = []

    def chunk_copy(chunk):
        rows = white_rt.at[pl.ds(chunk * LANES, LANES)]
        return remote(rows, rows, g_fwd.at[chunk], g_recv.at[chunk], sibling)

    for chunk in range(CHUNKS):
        owner = owner_of(chunk)
        relay = jnp.logical_and(c != owner, k == owner % 2)
        copy = chunk_copy(chunk)
        forwards.append((relay, copy))

        @pl.when(relay)
        def _():
            copy.wait_recv()
            copy.start()

    for chunk in range(CHUNKS):
        @pl.when(k != owner_of(chunk) % 2)
        def _():
            chunk_copy(chunk).wait_recv()

    leave_rt = pltpu.make_async_copy(white_rt, rt_out, out_sem.at[0])
    leave_rt.start()
    jacobi = squares_over_epochs(white_rt[...])
    direction0 = probes[...] / jacobi / wide_row(center)
    residual1 = probes[...] - back_product(exchange_finish(0), white_rt[...])
    direction1 = wide_row(rho1 * rho0) * direction0 + wide_row(2.0 * rho1 / half) * (residual1 / jacobi)
    exchange_start(
        1, pack(pair_sum(jnp.dot(split(direction1), white_rt[...], preferred_element_type=F32)))
    )

    for other in (False, True):
        for steps in (-3, -1, 1, 3, 4):
            await_block(block_of(other, steps))
    white_c[...] = jnp.dot(
        filt[...], cbuf[...].reshape(EPOCHS, WIDTH), preferred_element_type=F32
    ).astype(BF16)

    leave_c = pltpu.make_async_copy(white_c, c_out, out_sem.at[1])
    leave_c.start()

    state[0] = residual1
    state[1] = wide_row(2.0 * rho2 / half) / jacobi
    state[2] = direction0 + direction1 + wide_row(rho2 * rho1) * direction1
    leave_state = pltpu.make_async_copy(state, state_out, out_sem.at[2])
    leave_state.start()

    for copy in sends:
        copy.wait_send()
    for relay, copy in forwards:
        pl.when(relay)(copy.wait_send)

    @pl.when(is_owner)
    def _():
        await_bytes(rs_send.at[pl.ds(0, SIDE - 1)], rs_ssem)
        await_bytes(white_rt.at[pl.ds(0, 8 * LANES)], g_send)
        await_bytes(probes.at[:, pl.ds(0, WIDTH - LANES)], p_send)

    @pl.when(jnp.logical_not(is_owner))
    def _():
        await_bytes(probes, p_send)

    kept = jnp.logical_and(is_owner, on_diagonal)

    @pl.when(kept)
    def _():
        await_bytes(design.at[:, pl.ds(0, WIDTH - LANES)], s_send)

    @pl.when(jnp.logical_not(kept))
    def _():
        await_bytes(design, s_send)

    await_bytes(ubuf.at[0, pl.ds(0, SIDE - 1)], u_send.at[0])
    leave_rt.wait()
    leave_c.wait()
    leave_state.wait()

    last[...] = exchange_finish(1)
    leave_last = pltpu.make_async_copy(last, last_out, out_sem.at[3])
    leave_last.start()
    await_bytes(ubuf.at[1, pl.ds(0, SIDE - 1)], u_send.at[1])
    leave_last.wait()


def tile_kernel(
    rt_in, c_in, state_in, last_in, tile_out, answer_out,
    white_rt, white_c, state, last, answer, rows, in_sem, out_sem,
):
    load_c = pltpu.make_async_copy(c_in, white_c, in_sem.at[0])
    load_c.start()
    loads, leaves = [], []
    for part in range(STEPS):
        here = pl.ds(part * STEP, STEP)
        loads.append(pltpu.make_async_copy(rt_in.at[here], white_rt.at[here], in_sem.at[3 + part]))
        leaves.append(pltpu.make_async_copy(rows.at[part], tile_out.at[here], out_sem.at[1 + part]))
        loads[part].start()
    load_state = pltpu.make_async_copy(state_in, state, in_sem.at[1])
    load_last = pltpu.make_async_copy(last_in, last, in_sem.at[2])
    load_state.start()
    load_last.start()
    load_c.wait()
    for part in range(STEPS):
        loads[part].wait()
        rows[part] = jnp.dot(
            white_rt[part * STEP : (part + 1) * STEP], white_c[...], preferred_element_type=F32
        )
        leaves[part].start()
    load_state.wait()
    load_last.wait()
    residual2 = state[0] - back_product(last[...], white_rt[...])
    answer[...] = state[2] + state[1] * residual2
    leave_answer = pltpu.make_async_copy(answer, answer_out, out_sem.at[0])
    leave_answer.start()
    for leave in leaves:
        leave.wait()
    leave_answer.wait()


def body(design, filter_taps, probes, lower_bound, upper_bound):
    smem = pl.BlockSpec(memory_space=pltpu.SMEM)
    hbm = pl.BlockSpec(memory_space=pltpu.HBM)
    dma = pltpu.SemaphoreType.DMA
    held = pl.pallas_call(
        kernel,
        out_shape=(
            jax.ShapeDtypeStruct((WIDTH, EPOCHS), BF16),
            jax.ShapeDtypeStruct((EPOCHS, WIDTH), BF16),
            jax.ShapeDtypeStruct((3, 8, WIDTH), F32),
            jax.ShapeDtypeStruct((16, EPOCHS), BF16),
        ),
        in_specs=[hbm, hbm, hbm, smem, smem],
        out_specs=(hbm, hbm, hbm, hbm),
        scratch_shapes=[
            pltpu.VMEM((3, 8, WIDTH), F32),
            pltpu.VMEM((16, EPOCHS), BF16),
            pltpu.VMEM((BLOCK, WIDTH), BF16),
            pltpu.VMEM((1, EPOCHS), F32),
            pltpu.VMEM((8, WIDTH), F32),
            pltpu.VMEM((SIDE, BLOCK, WIDTH), BF16),
            pltpu.VMEM((SIDE, BLOCK, LANES), BF16),
            pltpu.VMEM((SIDE, 8, LANES), F32),
            pltpu.VMEM((EPOCHS, EPOCHS), BF16),
            pltpu.VMEM((EPOCHS, EPOCHS), BF16),
            pltpu.VMEM((WIDTH, EPOCHS), BF16),
            pltpu.VMEM((EPOCHS, WIDTH), BF16),
            pltpu.VMEM((2, 16, LANES), BF16),
            pltpu.VMEM((2, SIDE, 16, LANES), BF16),
            pltpu.VMEM((SIDE, 16, LANES), BF16),
            pltpu.VMEM((CHUNKS, 16, LANES), BF16),
            dma((3,)), dma((4,)),
            dma((15,)), dma((SIDE,)),
            dma, dma,
            dma, dma,
            dma, dma,
            dma, dma((CHUNKS,)), dma((CHUNKS,)),
            dma((2,)), dma((2,)),
        ],
        compiler_params=pltpu.CompilerParams(
            collective_id=1, has_side_effects=True, vmem_limit_bytes=GRANT
        ),
        name="gather_and_solve",
    )(design, filter_taps.reshape(1, EPOCHS), probes.T, lower_bound, upper_bound)
    tile, answer = pl.pallas_call(
        tile_kernel,
        out_shape=(
            jax.ShapeDtypeStruct((WIDTH, WIDTH), F32),
            jax.ShapeDtypeStruct((8, WIDTH), F32),
        ),
        in_specs=[hbm] * 4,
        out_specs=(hbm, hbm),
        scratch_shapes=[
            pltpu.VMEM((WIDTH, EPOCHS), BF16),
            pltpu.VMEM((EPOCHS, WIDTH), BF16),
            pltpu.VMEM((3, 8, WIDTH), F32),
            pltpu.VMEM((16, EPOCHS), BF16),
            pltpu.VMEM((8, WIDTH), F32),
            pltpu.VMEM((STEPS, STEP, WIDTH), F32),
            dma((3 + STEPS,)), dma((1 + STEPS,)),
        ],
        compiler_params=pltpu.CompilerParams(vmem_limit_bytes=GRANT),
        name="normal_tile",
    )(*held)
    return tile, answer.T


def solution(mesh):
    placed = (P("row", "col"), P(), P("row", "col"), P(), P())
    return jax.shard_map(
        body,
        mesh=mesh,
        in_specs=placed,
        out_specs=(P("row", "col"), P("row", "col")),
        check_vma=False,
    )
```

```python
import jax
import jax.numpy as jnp
from jax import lax
from jax.experimental import pallas as pl
from jax.experimental.pallas import tpu as pltpu
from jax.sharding import PartitionSpec as P

MESH = pl.DeviceIdType.MESH
F32 = jnp.float32
BF16 = jnp.bfloat16
EPOCHS = 256
SIDE = 16
BLOCK = 16
WIDTH = 1536
LANES = 128
CHUNKS = WIDTH // LANES
STEP = 256
STEPS = WIDTH // STEP
GRANT = 54 << 20
FIRST = (((0,), (0,)), ((), ()))
LAST = (((1,), (1,)), ((), ()))


def owner_of(chunk):
    return (chunk // 3) * 4 + chunk % 3


PLANE = tuple(sorted(((a, b) for a in range(2) for b in range(8) if a or b), key=lambda p: -(2 * p[0] + min(p[1], 8 - p[1]))))
ROW = tuple(
    sorted(
        ((a, b, d) for a in range(2) for b in range(4) for d in range(2) if a or b or d),
        key=lambda p: -(2 * (p[0] + min(p[1], 4 - p[1])) + p[2]),
    )
)


def remote(src, dst, send, recv, device):
    return pltpu.make_async_remote_copy(
        src_ref=src, dst_ref=dst, send_sem=send, recv_sem=recv, device_id=device, device_id_type=MESH
    )


def split(value):
    high = value.astype(BF16)
    low = (value - high.astype(F32)).astype(BF16)
    return jnp.concatenate([high, low], axis=0)


def pair_sum(value):
    rows = value.shape[0] // 2
    return value[:rows] + value[rows:]


def squares_over_epochs(transposed):
    wide = transposed.astype(F32)
    parts = split(wide * wide)
    rows = transposed.shape[0]
    ones = jnp.ones((8, EPOCHS), BF16)
    both = lax.dot_general(ones, parts, LAST, preferred_element_type=F32)
    return both[:, :rows] + both[:, rows:] + 1e-06


def pack(value):
    return jnp.concatenate([value[:, :LANES], value[:, LANES:]], axis=0).astype(BF16)


def back_product(whole, transposed):
    return pair_sum(lax.dot_general(whole, transposed, LAST, preferred_element_type=F32))


def plane_sum(slots):
    total = jnp.sum(slots.astype(F32), axis=0)
    return split(jnp.concatenate([total[:8], total[8:]], axis=1))


def kernel(
    design_in, taps_in, probes_in, lower, upper,
    rt_out, c_out, state_out, last_out,
    state, design, taps, probes,
    cbuf, rsub, psub, filt, filt_t, white_rt, white_c, usend, ubuf, rs_send, rs_buf,
    in_sem, out_sem, c_send, c_recv, s_send, s_recv, p_send, p_recv, rs_ssem, rs_rsem,
    g_send, g_fwd, g_recv, u_send, u_recv,
):
    r, c = lax.axis_index("row"), lax.axis_index("col")
    h, z = r // 8, r % 8
    l, x, k = c // 8, (c // 2) % 4, c % 2
    sibling = (r, c + 1 - 2 * k)
    z_next, z_prev = (h * 8 + (z + 1) % 8, c), (h * 8 + (z + 7) % 8, c)
    partner = ((1 - h) * 8 + z, c)
    is_owner = c % 4 != 3
    mine = (c // 4) * 3 + c % 4
    on_diagonal = r == c

    def in_plane(place):
        return ((h + place[0]) % 2) * 8 + (z + place[1]) % 8

    def in_row(place):
        return ((l + place[0]) % 2) * 8 + ((x + place[1]) % 4) * 2 + (k + place[2]) % 2

    loads = [
        pltpu.make_async_copy(src, dst, in_sem.at[i])
        for i, (src, dst) in enumerate(((design_in, design), (taps_in, taps), (probes_in, probes)))
    ]
    for load in loads:
        load.start()

    barrier = pltpu.get_barrier_semaphore()
    for place in PLANE:
        pl.semaphore_signal(barrier, inc=1, device_id=(in_plane(place), r), device_id_type=MESH)

    @pl.when(jnp.logical_not(on_diagonal))
    def _():
        pl.semaphore_signal(barrier, inc=1, device_id=(r, r), device_id_type=MESH)

    for place in PLANE:
        pl.semaphore_signal(barrier, inc=1, device_id=(in_plane(place), c), device_id_type=MESH)
    for place in ROW:
        pl.semaphore_signal(barrier, inc=1, device_id=(r, in_row(place)), device_id_type=MESH)

    loads[1].wait()
    shape = (EPOCHS, EPOCHS)
    row_id = lax.broadcasted_iota(jnp.int32, shape, 0)
    col_id = lax.broadcasted_iota(jnp.int32, shape, 1)
    moved = jnp.broadcast_to(taps[...], shape)
    for bit in range(8):
        moved = jnp.where((row_id >> bit) % 2 == 1, pltpu.roll(moved, 1 << bit, 1), moved)
    moved = jnp.where(col_id >= row_id, moved, 0.0) + jnp.where(col_id == row_id, 1.0, 0.0)
    filt_t[...] = moved.astype(BF16)
    filt[...] = moved.T.astype(BF16)

    low = jnp.full((1, LANES), lower[0], F32)
    high = jnp.full((1, LANES), upper[0], F32)
    center = (low + high) / 2.0
    half = (high - low) / 2.0
    sigma = center / half
    rho0 = 1.0 / sigma
    rho1 = 1.0 / (2.0 * sigma - rho0)
    rho2 = 1.0 / (2.0 * sigma - rho1)

    def await_bytes(ref, sem):
        pltpu.make_async_copy(ref, ref, sem).wait()

    def wide_row(row):
        return jnp.concatenate([row] * CHUNKS, axis=1)

    loads[0].wait()
    loads[2].wait()
    pl.semaphore_wait(barrier, 15 + 15 + 15 + jnp.where(on_diagonal, 0, 1))

    for chunk in range(CHUNKS):
        owner = owner_of(chunk)
        copy = remote(
            design.at[:, pl.ds(chunk * LANES, LANES)], rsub.at[r], s_send, s_recv, (c, owner)
        )
        away = jnp.logical_not(jnp.logical_and(on_diagonal, c == owner))

        @pl.when(away)
        def _():
            copy.start()

        @pl.when(jnp.logical_not(away))
        def _():
            rsub[r] = design[:, chunk * LANES : (chunk + 1) * LANES]

    def block_of(other, steps):
        return ((1 - h) if other else h) * 8 + (z + steps + 16) % 8

    sends = []

    def ship(slot, block, to, src=None):
        copy = remote(
            cbuf.at[block] if src is None else src, cbuf.at[block], c_send.at[slot], c_recv.at[block], to
        )
        copy.start()
        sends.append(copy)

    def await_block(block):
        remote(cbuf.at[block], cbuf.at[block], c_send.at[0], c_recv.at[block], z_next).wait_recv()

    way = 1 - 2 * h

    def at(steps):
        return (h * 8 + (z + steps + 8) % 8, c)

    ship(0, r, at(1), design)
    ship(1, r, at(-1), design)
    ship(2, r, partner, design)
    ship(3, r, at(2), design)
    ship(4, r, at(-2), design)
    for chunk in range(CHUNKS):
        owner = owner_of(chunk)
        copy = remote(
            probes.at[:, pl.ds(chunk * LANES, LANES)], psub.at[c], p_send, p_recv, (r, owner)
        )
        away = c != owner

        @pl.when(away)
        def _():
            copy.start()

        @pl.when(jnp.logical_not(away))
        def _():
            psub[c] = probes[:, chunk * LANES : (chunk + 1) * LANES]

    cbuf[r] = design[...]

    await_block(block_of(True, 0))
    ship(5, block_of(True, 0), at(1))
    ship(6, block_of(True, 0), at(-1))
    ship(7, block_of(True, 0), at(2))
    ship(8, block_of(True, 0), at(-2))
    my_rows = pl.ds(pl.multiple_of(mine * LANES, LANES), LANES)

    @pl.when(is_owner)
    def _():
        await_bytes(psub.at[pl.ds(0, SIDE - 1)], p_recv)
        right = psub[...].reshape(SIDE * 8, LANES) / center

        @pl.when(on_diagonal)
        def _():
            await_bytes(rsub.at[pl.ds(0, SIDE - 1)], s_recv)

        @pl.when(jnp.logical_not(on_diagonal))
        def _():
            await_bytes(rsub, s_recv)

        raw = rsub[...].reshape(EPOCHS, LANES)
        chunk_t = lax.dot_general(raw, filt_t[...], FIRST, preferred_element_type=F32).astype(BF16)
        wide = jnp.dot(filt[...], raw, preferred_element_type=F32).astype(BF16).astype(F32)
        jacobi = jnp.sum(wide * wide, axis=0, keepdims=True) + 1e-06
        part = pair_sum(jnp.dot(split(right / jacobi), chunk_t, preferred_element_type=F32))
        left = part[:, :LANES].reshape(SIDE, 8, LANES)
        right = part[:, LANES:].reshape(SIDE, 8, LANES)
        rs_send[...] = jnp.concatenate([left, right], axis=1).astype(BF16)
        for place in ROW:
            to = in_row(place)
            remote(rs_send.at[to], rs_buf.at[mine], rs_ssem, rs_rsem, (r, to)).start()
        rs_buf[mine] = rs_send[c]
        white_rt[my_rows, :] = chunk_t
        for place in ROW:
            if not place[2]:
                remote(
                    white_rt.at[my_rows], white_rt.at[my_rows], g_send, g_recv.at[mine], (r, in_row(place))
                ).start()
        remote(white_rt.at[my_rows], white_rt.at[my_rows], g_send, g_recv.at[mine], sibling).start()

    await_block(block_of(False, -2))
    ship(9, block_of(False, -2), at(1))
    await_block(block_of(False, 2))
    ship(10, block_of(False, 2), at(-1))
    ship(11, block_of(False, -2 * way), at(2 * way))
    await_block(block_of(True, -2))
    ship(12, block_of(True, -2), at(1))
    await_block(block_of(True, 2))
    ship(13, block_of(True, 2), at(-1))
    ship(14, block_of(True, 2 * way), at(-2 * way))
    def exchange_start(turn, packed, slots):
        usend[turn] = packed
        for place in PLANE:
            remote(
                usend.at[turn], slots.at[r], u_send.at[turn], u_recv.at[turn], (in_plane(place), c)
            ).start()

    @pl.when(is_owner)
    def _():
        await_bytes(rs_buf.at[pl.ds(0, CHUNKS - 1)], rs_rsem)

    @pl.when(jnp.logical_not(is_owner))
    def _():
        await_bytes(rs_buf, rs_rsem)

    summed = jnp.sum(rs_buf[...].astype(F32), axis=0).astype(BF16)
    exchange_start(0, summed, ubuf)
    ubuf[r] = summed

    forwards = []

    def chunk_copy(chunk):
        rows = white_rt.at[pl.ds(chunk * LANES, LANES)]
        return remote(rows, rows, g_fwd.at[chunk], g_recv.at[chunk], sibling)

    for chunk in range(CHUNKS):
        owner = owner_of(chunk)
        relay = jnp.logical_and(c != owner, k == owner % 2)
        copy = chunk_copy(chunk)
        forwards.append((relay, copy))

        @pl.when(relay)
        def _():
            copy.wait_recv()
            copy.start()

    for chunk in range(CHUNKS):
        @pl.when(k != owner_of(chunk) % 2)
        def _():
            chunk_copy(chunk).wait_recv()

    leave_rt = pltpu.make_async_copy(white_rt, rt_out, out_sem.at[0])
    leave_rt.start()
    jacobi = squares_over_epochs(white_rt[...])
    direction0 = probes[...] / jacobi / wide_row(center)
    await_bytes(ubuf.at[pl.ds(0, SIDE - 1)], u_recv.at[0])
    residual1 = probes[...] - back_product(plane_sum(ubuf[...]), white_rt[...])
    direction1 = wide_row(rho1 * rho0) * direction0 + wide_row(2.0 * rho1 / half) * (residual1 / jacobi)
    exchange_start(
        1, pack(pair_sum(jnp.dot(split(direction1), white_rt[...], preferred_element_type=F32))), last_out
    )
    keep_last = pltpu.make_async_copy(usend.at[1], last_out.at[r], out_sem.at[3])
    keep_last.start()

    for other in (False, True):
        for steps in (-3, -1, 1, 3, 4):
            await_block(block_of(other, steps))
    white_c[...] = jnp.dot(
        filt[...], cbuf[...].reshape(EPOCHS, WIDTH), preferred_element_type=F32
    ).astype(BF16)

    leave_c = pltpu.make_async_copy(white_c, c_out, out_sem.at[1])
    leave_c.start()

    state[0] = residual1
    state[1] = wide_row(2.0 * rho2 / half) / jacobi
    state[2] = direction0 + direction1 + wide_row(rho2 * rho1) * direction1
    leave_state = pltpu.make_async_copy(state, state_out, out_sem.at[2])
    leave_state.start()

    for copy in sends:
        copy.wait_send()
    for relay, copy in forwards:
        pl.when(relay)(copy.wait_send)

    @pl.when(is_owner)
    def _():
        await_bytes(rs_send.at[pl.ds(0, SIDE - 1)], rs_ssem)
        await_bytes(white_rt.at[pl.ds(0, 8 * LANES)], g_send)
        await_bytes(probes.at[:, pl.ds(0, WIDTH - LANES)], p_send)

    @pl.when(jnp.logical_not(is_owner))
    def _():
        await_bytes(probes, p_send)

    kept = jnp.logical_and(is_owner, on_diagonal)

    @pl.when(kept)
    def _():
        await_bytes(design.at[:, pl.ds(0, WIDTH - LANES)], s_send)

    @pl.when(jnp.logical_not(kept))
    def _():
        await_bytes(design, s_send)

    await_bytes(ubuf.at[pl.ds(0, SIDE - 1)], u_send.at[0])
    leave_rt.wait()
    leave_c.wait()
    leave_state.wait()

    keep_last.wait()
    await_bytes(ubuf.at[pl.ds(0, SIDE - 1)], u_send.at[1])
    await_bytes(ubuf.at[pl.ds(0, SIDE - 1)], u_recv.at[1])


def tile_kernel(
    rt_in, c_in, state_in, last_in, tile_out, answer_out,
    white_rt, white_c, state, last, answer, rows, in_sem, out_sem,
):
    load_c = pltpu.make_async_copy(c_in, white_c, in_sem.at[0])
    load_c.start()
    loads, leaves = [], []
    for part in range(STEPS):
        here = pl.ds(part * STEP, STEP)
        loads.append(pltpu.make_async_copy(rt_in.at[here], white_rt.at[here], in_sem.at[3 + part]))
        leaves.append(pltpu.make_async_copy(rows.at[part], tile_out.at[here], out_sem.at[1 + part]))
        loads[part].start()
    load_state = pltpu.make_async_copy(state_in, state, in_sem.at[1])
    load_last = pltpu.make_async_copy(last_in, last, in_sem.at[2])
    load_state.start()
    load_last.start()
    load_c.wait()
    for part in range(STEPS):
        loads[part].wait()
        rows[part] = jnp.dot(
            white_rt[part * STEP : (part + 1) * STEP], white_c[...], preferred_element_type=F32
        )
        leaves[part].start()
    load_state.wait()
    load_last.wait()
    residual2 = state[0] - back_product(plane_sum(last[...]), white_rt[...])
    answer[...] = state[2] + state[1] * residual2
    leave_answer = pltpu.make_async_copy(answer, answer_out, out_sem.at[0])
    leave_answer.start()
    for leave in leaves:
        leave.wait()
    leave_answer.wait()


def body(design, filter_taps, probes, lower_bound, upper_bound):
    smem = pl.BlockSpec(memory_space=pltpu.SMEM)
    hbm = pl.BlockSpec(memory_space=pltpu.HBM)
    dma = pltpu.SemaphoreType.DMA
    held = pl.pallas_call(
        kernel,
        out_shape=(
            jax.ShapeDtypeStruct((WIDTH, EPOCHS), BF16),
            jax.ShapeDtypeStruct((EPOCHS, WIDTH), BF16),
            jax.ShapeDtypeStruct((3, 8, WIDTH), F32),
            jax.ShapeDtypeStruct((SIDE, 16, LANES), BF16),
        ),
        in_specs=[hbm, hbm, hbm, smem, smem],
        out_specs=(hbm, hbm, hbm, hbm),
        scratch_shapes=[
            pltpu.VMEM((3, 8, WIDTH), F32),
            pltpu.VMEM((BLOCK, WIDTH), BF16),
            pltpu.VMEM((1, EPOCHS), F32),
            pltpu.VMEM((8, WIDTH), F32),
            pltpu.VMEM((SIDE, BLOCK, WIDTH), BF16),
            pltpu.VMEM((SIDE, BLOCK, LANES), BF16),
            pltpu.VMEM((SIDE, 8, LANES), F32),
            pltpu.VMEM((EPOCHS, EPOCHS), BF16),
            pltpu.VMEM((EPOCHS, EPOCHS), BF16),
            pltpu.VMEM((WIDTH, EPOCHS), BF16),
            pltpu.VMEM((EPOCHS, WIDTH), BF16),
            pltpu.VMEM((2, 16, LANES), BF16),
            pltpu.VMEM((SIDE, 16, LANES), BF16),
            pltpu.VMEM((SIDE, 16, LANES), BF16),
            pltpu.VMEM((CHUNKS, 16, LANES), BF16),
            dma((3,)), dma((4,)),
            dma((15,)), dma((SIDE,)),
            dma, dma,
            dma, dma,
            dma, dma,
            dma, dma((CHUNKS,)), dma((CHUNKS,)),
            dma((2,)), dma((2,)),
        ],
        compiler_params=pltpu.CompilerParams(
            collective_id=1, has_side_effects=True, vmem_limit_bytes=GRANT
        ),
        name="gather_and_solve",
    )(design, filter_taps.reshape(1, EPOCHS), probes.T, lower_bound, upper_bound)
    tile, answer = pl.pallas_call(
        tile_kernel,
        out_shape=(
            jax.ShapeDtypeStruct((WIDTH, WIDTH), F32),
            jax.ShapeDtypeStruct((8, WIDTH), F32),
        ),
        in_specs=[hbm] * 4,
        out_specs=(hbm, hbm),
        scratch_shapes=[
            pltpu.VMEM((WIDTH, EPOCHS), BF16),
            pltpu.VMEM((EPOCHS, WIDTH), BF16),
            pltpu.VMEM((3, 8, WIDTH), F32),
            pltpu.VMEM((SIDE, 16, LANES), BF16),
            pltpu.VMEM((8, WIDTH), F32),
            pltpu.VMEM((STEPS, STEP, WIDTH), F32),
            dma((3 + STEPS,)), dma((1 + STEPS,)),
        ],
        compiler_params=pltpu.CompilerParams(vmem_limit_bytes=GRANT),
        name="normal_tile",
    )(*held)
    return tile, answer.T


def solution(mesh):
    placed = (P("row", "col"), P(), P("row", "col"), P(), P())
    return jax.shard_map(
        body,
        mesh=mesh,
        in_specs=placed,
        out_specs=(P("row", "col"), P("row", "col")),
        check_vma=False,
    )
```

```python
import jax
import jax.numpy as jnp
from jax import lax
from jax.experimental import pallas as pl
from jax.experimental.pallas import tpu as pltpu
from jax.sharding import PartitionSpec as P

MESH = pl.DeviceIdType.MESH
F32 = jnp.float32
BF16 = jnp.bfloat16
EPOCHS = 256
SIDE = 16
BLOCK = 16
WIDTH = 1536
LANES = 128
CHUNKS = WIDTH // LANES
STEP = 256
STEPS = WIDTH // STEP
GRANT = 54 << 20
FIRST = (((0,), (0,)), ((), ()))
LAST = (((1,), (1,)), ((), ()))


ASIDE = (1, 3, 0)


def owner_of(chunk, start):
    return ((chunk // 2) % 2) * 8 + ((start + ASIDE[chunk // 4]) % 4) * 2 + chunk % 2


PLANE = tuple(sorted(((a, b) for a in range(2) for b in range(8) if a or b), key=lambda p: -(2 * p[0] + min(p[1], 8 - p[1]))))
ROW = tuple(
    sorted(
        ((a, b, d) for a in range(2) for b in range(4) for d in range(2) if a or b or d),
        key=lambda p: -(2 * (p[0] + min(p[1], 4 - p[1])) + p[2]),
    )
)


def remote(src, dst, send, recv, device):
    return pltpu.make_async_remote_copy(
        src_ref=src, dst_ref=dst, send_sem=send, recv_sem=recv, device_id=device, device_id_type=MESH
    )


def split(value):
    high = value.astype(BF16)
    low = (value - high.astype(F32)).astype(BF16)
    return jnp.concatenate([high, low], axis=0)


def pair_sum(value):
    rows = value.shape[0] // 2
    return value[:rows] + value[rows:]


def squares_over_epochs(transposed):
    wide = transposed.astype(F32)
    parts = split(wide * wide)
    rows = transposed.shape[0]
    ones = jnp.ones((8, EPOCHS), BF16)
    both = lax.dot_general(ones, parts, LAST, preferred_element_type=F32)
    return both[:, :rows] + both[:, rows:] + 1e-06


def pack(value):
    return jnp.concatenate([value[:, :LANES], value[:, LANES:]], axis=0).astype(BF16)


def back_product(whole, transposed):
    return pair_sum(lax.dot_general(whole, transposed, LAST, preferred_element_type=F32))


def plane_sum(slots):
    total = jnp.sum(slots.astype(F32), axis=0)
    return split(jnp.concatenate([total[:8], total[8:]], axis=1))


def kernel(
    design_in, taps_in, probes_in, lower, upper,
    rt_out, c_out, state_out, last_out,
    state, jac, design, taps, probes,
    cbuf, rsub, psub, filt, filt_t, white_rt, white_c, usend, ubuf, rs_send, rs_buf,
    in_sem, out_sem, c_send, c_recv, s_send, s_recv, p_send, p_recv, rs_ssem, rs_rsem,
    g_send, g_fwd, g_recv, u_send, u_recv,
):
    r, c = lax.axis_index("row"), lax.axis_index("col")
    h, z = r // 8, r % 8
    l, x, k = c // 8, (c // 2) % 4, c % 2
    sibling = (r, c + 1 - 2 * k)
    z_next, z_prev = (h * 8 + (z + 1) % 8, c), (h * 8 + (z + 7) % 8, c)
    partner = ((1 - h) * 8 + z, c)
    start = z // 2
    aside = (x - start + 4) % 4
    is_owner = aside != 2
    mine = jnp.where(aside == 1, 0, jnp.where(aside == 3, 1, 2)) * 4 + l * 2 + k
    on_diagonal = r == c

    def in_plane(place):
        return ((h + place[0]) % 2) * 8 + (z + place[1]) % 8

    def in_row(place):
        return ((l + place[0]) % 2) * 8 + ((x + place[1]) % 4) * 2 + (k + place[2]) % 2

    loads = [
        pltpu.make_async_copy(src, dst, in_sem.at[i])
        for i, (src, dst) in enumerate(((design_in, design), (taps_in, taps), (probes_in, probes)))
    ]
    for load in loads:
        load.start()

    barrier = pltpu.get_barrier_semaphore()
    @pl.when(is_owner)
    def _():
        for place in PLANE:
            pl.semaphore_signal(barrier, inc=1, device_id=(in_plane(place), r), device_id_type=MESH)

        @pl.when(jnp.logical_not(on_diagonal))
        def _():
            pl.semaphore_signal(barrier, inc=1, device_id=(r, r), device_id_type=MESH)

    for place in PLANE:
        pl.semaphore_signal(barrier, inc=1, device_id=(in_plane(place), c), device_id_type=MESH)
    for place in ROW:
        pl.semaphore_signal(barrier, inc=1, device_id=(r, in_row(place)), device_id_type=MESH)

    loads[1].wait()
    shape = (EPOCHS, EPOCHS)
    row_id = lax.broadcasted_iota(jnp.int32, shape, 0)
    col_id = lax.broadcasted_iota(jnp.int32, shape, 1)
    moved = jnp.broadcast_to(taps[...], shape)
    for bit in range(8):
        moved = jnp.where((row_id >> bit) % 2 == 1, pltpu.roll(moved, 1 << bit, 1), moved)
    moved = jnp.where(col_id >= row_id, moved, 0.0) + jnp.where(col_id == row_id, 1.0, 0.0)
    filt_t[...] = moved.astype(BF16)
    filt[...] = moved.T.astype(BF16)

    low = jnp.full((1, LANES), lower[0], F32)
    high = jnp.full((1, LANES), upper[0], F32)
    center = (low + high) / 2.0
    half = (high - low) / 2.0
    sigma = center / half
    rho0 = 1.0 / sigma
    rho1 = 1.0 / (2.0 * sigma - rho0)
    rho2 = 1.0 / (2.0 * sigma - rho1)

    def await_bytes(ref, sem):
        pltpu.make_async_copy(ref, ref, sem).wait()

    def wide_row(row):
        return jnp.concatenate([row] * CHUNKS, axis=1)

    loads[0].wait()
    loads[2].wait()
    pl.semaphore_wait(barrier, 15 + 15 + CHUNKS - jnp.where(on_diagonal, 1, 0))

    for chunk in range(CHUNKS):
        owner = owner_of(chunk, x)
        copy = remote(
            design.at[:, pl.ds(chunk * LANES, LANES)], rsub.at[r], s_send, s_recv, (c, owner)
        )
        away = jnp.logical_not(jnp.logical_and(on_diagonal, c == owner))

        @pl.when(away)
        def _():
            copy.start()

        @pl.when(jnp.logical_not(away))
        def _():
            rsub[r] = design[:, chunk * LANES : (chunk + 1) * LANES]

    def block_of(other, steps):
        return ((1 - h) if other else h) * 8 + (z + steps + 16) % 8

    sends = []

    def ship(slot, block, to, src=None):
        copy = remote(
            cbuf.at[block] if src is None else src, cbuf.at[block], c_send.at[slot], c_recv.at[block], to
        )
        copy.start()
        sends.append(copy)

    def await_block(block):
        remote(cbuf.at[block], cbuf.at[block], c_send.at[0], c_recv.at[block], z_next).wait_recv()

    way = 1 - 2 * h

    def at(steps):
        return (h * 8 + (z + steps + 8) % 8, c)

    ship(0, r, at(1), design)
    ship(1, r, at(-1), design)
    ship(2, r, partner, design)
    ship(3, r, at(2), design)
    ship(4, r, at(-2), design)
    for chunk in range(CHUNKS):
        owner = owner_of(chunk, start)
        copy = remote(
            probes.at[:, pl.ds(chunk * LANES, LANES)], psub.at[c], p_send, p_recv, (r, owner)
        )
        away = c != owner

        @pl.when(away)
        def _():
            copy.start()

        @pl.when(jnp.logical_not(away))
        def _():
            psub[c] = probes[:, chunk * LANES : (chunk + 1) * LANES]

    cbuf[r] = design[...]

    await_block(block_of(True, 0))
    ship(5, block_of(True, 0), at(1))
    ship(6, block_of(True, 0), at(-1))
    ship(7, block_of(True, 0), at(2))
    ship(8, block_of(True, 0), at(-2))
    my_rows = pl.ds(pl.multiple_of(mine * LANES, LANES), LANES)

    @pl.when(is_owner)
    def _():
        await_bytes(psub.at[pl.ds(0, SIDE - 1)], p_recv)
        right = psub[...].reshape(SIDE * 8, LANES) / center

        @pl.when(on_diagonal)
        def _():
            await_bytes(rsub.at[pl.ds(0, SIDE - 1)], s_recv)

        @pl.when(jnp.logical_not(on_diagonal))
        def _():
            await_bytes(rsub, s_recv)

        raw = rsub[...].reshape(EPOCHS, LANES)
        chunk_t = lax.dot_general(raw, filt_t[...], FIRST, preferred_element_type=F32).astype(BF16)
        wide = jnp.dot(filt[...], raw, preferred_element_type=F32).astype(BF16).astype(F32)
        jacobi = jnp.sum(wide * wide, axis=0, keepdims=True) + 1e-06
        part = pair_sum(jnp.dot(split(right / jacobi), chunk_t, preferred_element_type=F32))
        left = part[:, :LANES].reshape(SIDE, 8, LANES)
        right = part[:, LANES:].reshape(SIDE, 8, LANES)
        rs_send[...] = jnp.concatenate([left, right], axis=1).astype(BF16)
        for place in ROW:
            to = in_row(place)
            remote(rs_send.at[to], rs_buf.at[mine], rs_ssem, rs_rsem, (r, to)).start()
        rs_buf[mine] = rs_send[c]
        white_rt[my_rows, :] = chunk_t
        for place in ROW:
            if not place[2]:
                remote(
                    white_rt.at[my_rows], white_rt.at[my_rows], g_send, g_recv.at[mine], (r, in_row(place))
                ).start()
        remote(white_rt.at[my_rows], white_rt.at[my_rows], g_send, g_recv.at[mine], sibling).start()

    await_block(block_of(False, -2))
    ship(9, block_of(False, -2), at(1))
    await_block(block_of(False, 2))
    ship(10, block_of(False, 2), at(-1))
    ship(11, block_of(False, -2 * way), at(2 * way))
    await_block(block_of(True, -2))
    ship(12, block_of(True, -2), at(1))
    await_block(block_of(True, 2))
    ship(13, block_of(True, 2), at(-1))
    ship(14, block_of(True, 2 * way), at(-2 * way))
    def exchange_start(turn, packed, slots):
        usend[turn] = packed
        for place in PLANE:
            remote(
                usend.at[turn], slots.at[r], u_send.at[turn], u_recv.at[turn], (in_plane(place), c)
            ).start()

    @pl.when(is_owner)
    def _():
        await_bytes(rs_buf.at[pl.ds(0, CHUNKS - 1)], rs_rsem)

    @pl.when(jnp.logical_not(is_owner))
    def _():
        await_bytes(rs_buf, rs_rsem)

    summed = jnp.sum(rs_buf[...].astype(F32), axis=0).astype(BF16)
    exchange_start(0, summed, ubuf)
    ubuf[r] = summed

    forwards = []

    def rows_of(chunk):
        return pl.ds(pl.multiple_of(chunk * LANES, LANES), LANES)

    def chunk_copy(i, chunk):
        rows = white_rt.at[rows_of(chunk)]
        return remote(rows, rows, g_fwd.at[i], g_recv.at[chunk], sibling)

    def take_jacobi(chunk):
        jac[:, rows_of(chunk)] = squares_over_epochs(white_rt[rows_of(chunk), :])

    for i in range(CHUNKS // 2):
        relay = c != (i % 2) * 8 + ((start + ASIDE[i // 2]) % 4) * 2 + k
        copy = chunk_copy(i, 2 * i + k)
        forwards.append((relay, copy))

        @pl.when(relay)
        def _():
            copy.wait_recv()
            copy.start()

    for i in range(CHUNKS // 2):
        take_jacobi(2 * i + k)
    for i in range(CHUNKS // 2):
        chunk_copy(i, 2 * i + 1 - k).wait_recv()
        take_jacobi(2 * i + 1 - k)

    leave_rt = pltpu.make_async_copy(white_rt, rt_out, out_sem.at[0])
    leave_rt.start()
    jacobi = jac[...]
    direction0 = probes[...] / jacobi / wide_row(center)
    await_bytes(ubuf.at[pl.ds(0, SIDE - 1)], u_recv.at[0])
    residual1 = probes[...] - back_product(plane_sum(ubuf[...]), white_rt[...])
    direction1 = wide_row(rho1 * rho0) * direction0 + wide_row(2.0 * rho1 / half) * (residual1 / jacobi)
    exchange_start(
        1, pack(pair_sum(jnp.dot(split(direction1), white_rt[...], preferred_element_type=F32))), last_out
    )
    keep_last = pltpu.make_async_copy(usend.at[1], last_out.at[r], out_sem.at[3])
    keep_last.start()

    for other in (False, True):
        for steps in (-3, -1, 1, 3, 4):
            await_block(block_of(other, steps))
    white_c[...] = jnp.dot(
        filt[...], cbuf[...].reshape(EPOCHS, WIDTH), preferred_element_type=F32
    ).astype(BF16)

    leave_c = pltpu.make_async_copy(white_c, c_out, out_sem.at[1])
    leave_c.start()

    state[0] = residual1
    state[1] = wide_row(2.0 * rho2 / half) / jacobi
    state[2] = direction0 + direction1 + wide_row(rho2 * rho1) * direction1
    leave_state = pltpu.make_async_copy(state, state_out, out_sem.at[2])
    leave_state.start()

    for copy in sends:
        copy.wait_send()
    for relay, copy in forwards:
        pl.when(relay)(copy.wait_send)

    @pl.when(is_owner)
    def _():
        await_bytes(rs_send.at[pl.ds(0, SIDE - 1)], rs_ssem)
        await_bytes(white_rt.at[pl.ds(0, 8 * LANES)], g_send)
        await_bytes(probes.at[:, pl.ds(0, WIDTH - LANES)], p_send)

    @pl.when(jnp.logical_not(is_owner))
    def _():
        await_bytes(probes, p_send)

    kept = jnp.logical_and(is_owner, on_diagonal)

    @pl.when(kept)
    def _():
        await_bytes(design.at[:, pl.ds(0, WIDTH - LANES)], s_send)

    @pl.when(jnp.logical_not(kept))
    def _():
        await_bytes(design, s_send)

    await_bytes(ubuf.at[pl.ds(0, SIDE - 1)], u_send.at[0])
    leave_rt.wait()
    leave_c.wait()
    leave_state.wait()

    keep_last.wait()
    await_bytes(ubuf.at[pl.ds(0, SIDE - 1)], u_send.at[1])
    await_bytes(ubuf.at[pl.ds(0, SIDE - 1)], u_recv.at[1])


def tile_kernel(
    rt_in, c_in, state_in, last_in, tile_out, answer_out,
    white_rt, white_c, state, last, answer, rows, in_sem, out_sem,
):
    load_c = pltpu.make_async_copy(c_in, white_c, in_sem.at[0])
    load_c.start()
    loads, leaves = [], []
    for part in range(STEPS):
        here = pl.ds(part * STEP, STEP)
        loads.append(pltpu.make_async_copy(rt_in.at[here], white_rt.at[here], in_sem.at[3 + part]))
        leaves.append(pltpu.make_async_copy(rows.at[part], tile_out.at[here], out_sem.at[1 + part]))
        loads[part].start()
    load_state = pltpu.make_async_copy(state_in, state, in_sem.at[1])
    load_last = pltpu.make_async_copy(last_in, last, in_sem.at[2])
    load_state.start()
    load_last.start()
    load_c.wait()
    for part in range(STEPS):
        loads[part].wait()
        rows[part] = jnp.dot(
            white_rt[part * STEP : (part + 1) * STEP], white_c[...], preferred_element_type=F32
        )
        leaves[part].start()
    load_state.wait()
    load_last.wait()
    residual2 = state[0] - back_product(plane_sum(last[...]), white_rt[...])
    answer[...] = state[2] + state[1] * residual2
    leave_answer = pltpu.make_async_copy(answer, answer_out, out_sem.at[0])
    leave_answer.start()
    for leave in leaves:
        leave.wait()
    leave_answer.wait()


def body(design, filter_taps, probes, lower_bound, upper_bound):
    smem = pl.BlockSpec(memory_space=pltpu.SMEM)
    hbm = pl.BlockSpec(memory_space=pltpu.HBM)
    dma = pltpu.SemaphoreType.DMA
    held = pl.pallas_call(
        kernel,
        out_shape=(
            jax.ShapeDtypeStruct((WIDTH, EPOCHS), BF16),
            jax.ShapeDtypeStruct((EPOCHS, WIDTH), BF16),
            jax.ShapeDtypeStruct((3, 8, WIDTH), F32),
            jax.ShapeDtypeStruct((SIDE, 16, LANES), BF16),
        ),
        in_specs=[hbm, hbm, hbm, smem, smem],
        out_specs=(hbm, hbm, hbm, hbm),
        scratch_shapes=[
            pltpu.VMEM((3, 8, WIDTH), F32),
            pltpu.VMEM((8, WIDTH), F32),
            pltpu.VMEM((BLOCK, WIDTH), BF16),
            pltpu.VMEM((1, EPOCHS), F32),
            pltpu.VMEM((8, WIDTH), F32),
            pltpu.VMEM((SIDE, BLOCK, WIDTH), BF16),
            pltpu.VMEM((SIDE, BLOCK, LANES), BF16),
            pltpu.VMEM((SIDE, 8, LANES), F32),
            pltpu.VMEM((EPOCHS, EPOCHS), BF16),
            pltpu.VMEM((EPOCHS, EPOCHS), BF16),
            pltpu.VMEM((WIDTH, EPOCHS), BF16),
            pltpu.VMEM((EPOCHS, WIDTH), BF16),
            pltpu.VMEM((2, 16, LANES), BF16),
            pltpu.VMEM((SIDE, 16, LANES), BF16),
            pltpu.VMEM((SIDE, 16, LANES), BF16),
            pltpu.VMEM((CHUNKS, 16, LANES), BF16),
            dma((3,)), dma((4,)),
            dma((15,)), dma((SIDE,)),
            dma, dma,
            dma, dma,
            dma, dma,
            dma, dma((CHUNKS // 2,)), dma((CHUNKS,)),
            dma((2,)), dma((2,)),
        ],
        compiler_params=pltpu.CompilerParams(
            collective_id=1, has_side_effects=True, vmem_limit_bytes=GRANT
        ),
        name="gather_and_solve",
    )(design, filter_taps.reshape(1, EPOCHS), probes.T, lower_bound, upper_bound)
    tile, answer = pl.pallas_call(
        tile_kernel,
        out_shape=(
            jax.ShapeDtypeStruct((WIDTH, WIDTH), F32),
            jax.ShapeDtypeStruct((8, WIDTH), F32),
        ),
        in_specs=[hbm] * 4,
        out_specs=(hbm, hbm),
        scratch_shapes=[
            pltpu.VMEM((WIDTH, EPOCHS), BF16),
            pltpu.VMEM((EPOCHS, WIDTH), BF16),
            pltpu.VMEM((3, 8, WIDTH), F32),
            pltpu.VMEM((SIDE, 16, LANES), BF16),
            pltpu.VMEM((8, WIDTH), F32),
            pltpu.VMEM((STEPS, STEP, WIDTH), F32),
            dma((3 + STEPS,)), dma((1 + STEPS,)),
        ],
        compiler_params=pltpu.CompilerParams(vmem_limit_bytes=GRANT),
        name="normal_tile",
    )(*held)
    return tile, answer.T


def solution(mesh):
    placed = (P("row", "col"), P(), P("row", "col"), P(), P())
    return jax.shard_map(
        body,
        mesh=mesh,
        in_specs=placed,
        out_specs=(P("row", "col"), P("row", "col")),
        check_vma=False,
    )
```

```python
import jax
import jax.numpy as jnp
from jax import lax
from jax.experimental import pallas as pl
from jax.experimental.pallas import tpu as pltpu
from jax.sharding import PartitionSpec as P

MESH = pl.DeviceIdType.MESH
F32 = jnp.float32
BF16 = jnp.bfloat16
EPOCHS = 256
SIDE = 16
BLOCK = 16
WIDTH = 1536
LANES = 128
CHUNKS = WIDTH // LANES
STEP = 256
STEPS = WIDTH // STEP
GRANT = 54 << 20
FIRST = (((0,), (0,)), ((), ()))
LAST = (((1,), (1,)), ((), ()))


ASIDE = (1, 3, 0)


def owner_of(chunk, start):
    return ((chunk // 2) % 2) * 8 + ((start + ASIDE[chunk // 4]) % 4) * 2 + chunk % 2


PLANE = tuple(sorted(((a, b) for a in range(2) for b in range(8) if a or b), key=lambda p: -(2 * p[0] + min(p[1], 8 - p[1]))))
ROW = tuple(
    sorted(
        ((a, b, d) for a in range(2) for b in range(4) for d in range(2) if a or b or d),
        key=lambda p: -(2 * (p[0] + min(p[1], 4 - p[1])) + p[2]),
    )
)


def remote(src, dst, send, recv, device):
    return pltpu.make_async_remote_copy(
        src_ref=src, dst_ref=dst, send_sem=send, recv_sem=recv, device_id=device, device_id_type=MESH
    )


def split(value):
    high = value.astype(BF16)
    low = (value - high.astype(F32)).astype(BF16)
    return jnp.concatenate([high, low], axis=0)


def pair_sum(value):
    rows = value.shape[0] // 2
    return value[:rows] + value[rows:]


def squares_over_epochs(transposed):
    wide = transposed.astype(F32)
    parts = split(wide * wide)
    rows = transposed.shape[0]
    ones = jnp.ones((8, EPOCHS), BF16)
    both = lax.dot_general(ones, parts, LAST, preferred_element_type=F32)
    return both[:, :rows] + both[:, rows:] + 1e-06


def pack(value):
    return jnp.concatenate([value[:, :LANES], value[:, LANES:]], axis=0).astype(BF16)


def back_product(whole, transposed):
    return pair_sum(lax.dot_general(whole, transposed, LAST, preferred_element_type=F32))


def plane_sum(slots):
    total = jnp.sum(slots.astype(F32), axis=0)
    return split(jnp.concatenate([total[:8], total[8:]], axis=1))


def kernel(
    design_in, taps_in, probes_in, lower, upper,
    rt_out, c_out, state_out, last_out,
    state, jac, design, taps, probes,
    cbuf, rsub, psub, filt, filt_t, white_rt, white_c, usend, ubuf, rs_send, rs_buf,
    in_sem, out_sem, c_send, c_recv, s_send, s_recv, p_send, p_recv, rs_ssem, rs_rsem,
    g_send, g_fwd, g_recv, u_send, u_recv,
):
    r, c = lax.axis_index("row"), lax.axis_index("col")
    h, z = r // 8, r % 8
    l, x, k = c // 8, (c // 2) % 4, c % 2
    sibling = (r, c + 1 - 2 * k)
    z_next, z_prev = (h * 8 + (z + 1) % 8, c), (h * 8 + (z + 7) % 8, c)
    partner = ((1 - h) * 8 + z, c)
    start = z // 2
    aside = (x - start + 4) % 4
    is_owner = aside != 2
    mine = jnp.where(aside == 1, 0, jnp.where(aside == 3, 1, 2)) * 4 + l * 2 + k
    on_diagonal = r == c

    def in_plane(place):
        return ((h + place[0]) % 2) * 8 + (z + place[1]) % 8

    def in_row(place):
        return ((l + place[0]) % 2) * 8 + ((x + place[1]) % 4) * 2 + (k + place[2]) % 2

    loads = [
        pltpu.make_async_copy(src, dst, in_sem.at[i])
        for i, (src, dst) in enumerate(((design_in, design), (taps_in, taps), (probes_in, probes)))
    ]
    for load in loads:
        load.start()

    barrier = pltpu.get_barrier_semaphore()
    @pl.when(is_owner)
    def _():
        for place in PLANE:
            pl.semaphore_signal(barrier, inc=1, device_id=(in_plane(place), r), device_id_type=MESH)

        @pl.when(jnp.logical_not(on_diagonal))
        def _():
            pl.semaphore_signal(barrier, inc=1, device_id=(r, r), device_id_type=MESH)

    for place in PLANE:
        pl.semaphore_signal(barrier, inc=1, device_id=(in_plane(place), c), device_id_type=MESH)
    for place in ROW:
        pl.semaphore_signal(barrier, inc=1, device_id=(r, in_row(place)), device_id_type=MESH)

    loads[1].wait()
    shape = (EPOCHS, EPOCHS)
    row_id = lax.broadcasted_iota(jnp.int32, shape, 0)
    col_id = lax.broadcasted_iota(jnp.int32, shape, 1)
    moved = jnp.broadcast_to(taps[...], shape)
    for bit in range(8):
        moved = jnp.where((row_id >> bit) % 2 == 1, pltpu.roll(moved, 1 << bit, 1), moved)
    moved = jnp.where(col_id >= row_id, moved, 0.0) + jnp.where(col_id == row_id, 1.0, 0.0)
    filt_t[...] = moved.astype(BF16)
    filt[...] = moved.T.astype(BF16)

    low = jnp.full((1, LANES), lower[0], F32)
    high = jnp.full((1, LANES), upper[0], F32)
    center = (low + high) / 2.0
    half = (high - low) / 2.0
    sigma = center / half
    rho0 = 1.0 / sigma
    rho1 = 1.0 / (2.0 * sigma - rho0)
    rho2 = 1.0 / (2.0 * sigma - rho1)

    def await_bytes(ref, sem):
        pltpu.make_async_copy(ref, ref, sem).wait()

    def wide_row(row):
        return jnp.concatenate([row] * CHUNKS, axis=1)

    loads[0].wait()
    loads[2].wait()
    pl.semaphore_wait(barrier, 15 + 15 + CHUNKS - jnp.where(on_diagonal, 1, 0))

    for chunk in range(CHUNKS):
        owner = owner_of(chunk, x)
        copy = remote(
            design.at[:, pl.ds(chunk * LANES, LANES)], rsub.at[r], s_send, s_recv, (c, owner)
        )
        away = jnp.logical_not(jnp.logical_and(on_diagonal, c == owner))

        @pl.when(away)
        def _():
            copy.start()

        @pl.when(jnp.logical_not(away))
        def _():
            rsub[r] = design[:, chunk * LANES : (chunk + 1) * LANES]

    def block_of(other, steps):
        return ((1 - h) if other else h) * 8 + (z + steps + 16) % 8

    sends = []

    def ship(slot, block, to, src=None):
        copy = remote(
            cbuf.at[block] if src is None else src, cbuf.at[block], c_send.at[slot], c_recv.at[block], to
        )
        copy.start()
        sends.append(copy)

    def await_block(block):
        remote(cbuf.at[block], cbuf.at[block], c_send.at[0], c_recv.at[block], z_next).wait_recv()

    way = 1 - 2 * h

    def at(steps):
        return (h * 8 + (z + steps + 8) % 8, c)

    ship(2, r, partner, design)
    ship(3, r, at(2), design)
    ship(4, r, at(-2), design)
    ship(0, r, at(1), design)
    ship(1, r, at(-1), design)
    for chunk in range(CHUNKS):
        owner = owner_of(chunk, start)
        copy = remote(
            probes.at[:, pl.ds(chunk * LANES, LANES)], psub.at[c], p_send, p_recv, (r, owner)
        )
        away = c != owner

        @pl.when(away)
        def _():
            copy.start()

        @pl.when(jnp.logical_not(away))
        def _():
            psub[c] = probes[:, chunk * LANES : (chunk + 1) * LANES]

    cbuf[r] = design[...]

    await_block(block_of(True, 0))
    ship(7, block_of(True, 0), at(2))
    ship(8, block_of(True, 0), at(-2))
    ship(5, block_of(True, 0), at(1))
    ship(6, block_of(True, 0), at(-1))
    my_rows = pl.ds(pl.multiple_of(mine * LANES, LANES), LANES)

    @pl.when(is_owner)
    def _():
        await_bytes(psub.at[pl.ds(0, SIDE - 1)], p_recv)
        right = psub[...].reshape(SIDE * 8, LANES) / center

        @pl.when(on_diagonal)
        def _():
            await_bytes(rsub.at[pl.ds(0, SIDE - 1)], s_recv)

        @pl.when(jnp.logical_not(on_diagonal))
        def _():
            await_bytes(rsub, s_recv)

        raw = rsub[...].reshape(EPOCHS, LANES)
        chunk_t = lax.dot_general(raw, filt_t[...], FIRST, preferred_element_type=F32).astype(BF16)
        wide = jnp.dot(filt[...], raw, preferred_element_type=F32).astype(BF16).astype(F32)
        jacobi = jnp.sum(wide * wide, axis=0, keepdims=True) + 1e-06
        part = pair_sum(jnp.dot(split(right / jacobi), chunk_t, preferred_element_type=F32))
        left = part[:, :LANES].reshape(SIDE, 8, LANES)
        right = part[:, LANES:].reshape(SIDE, 8, LANES)
        rs_send[...] = jnp.concatenate([left, right], axis=1).astype(BF16)
        for place in ROW:
            to = in_row(place)
            remote(rs_send.at[to], rs_buf.at[mine], rs_ssem, rs_rsem, (r, to)).start()
        rs_buf[mine] = rs_send[c]
        white_rt[my_rows, :] = chunk_t
        for place in ROW:
            if not place[2]:
                remote(
                    white_rt.at[my_rows], white_rt.at[my_rows], g_send, g_recv.at[mine], (r, in_row(place))
                ).start()
        remote(white_rt.at[my_rows], white_rt.at[my_rows], g_send, g_recv.at[mine], sibling).start()

    def exchange_start(turn, packed, slots):
        usend[turn] = packed
        for place in PLANE:
            remote(
                usend.at[turn], slots.at[r], u_send.at[turn], u_recv.at[turn], (in_plane(place), c)
            ).start()

    @pl.when(is_owner)
    def _():
        await_bytes(rs_buf.at[pl.ds(0, CHUNKS - 1)], rs_rsem)

    @pl.when(jnp.logical_not(is_owner))
    def _():
        await_bytes(rs_buf, rs_rsem)

    summed = jnp.sum(rs_buf[...].astype(F32), axis=0).astype(BF16)
    exchange_start(0, summed, ubuf)
    ubuf[r] = summed

    await_block(block_of(False, -2))
    ship(9, block_of(False, -2), at(1))
    await_block(block_of(False, 2))
    ship(10, block_of(False, 2), at(-1))
    ship(11, block_of(False, -2 * way), at(2 * way))
    await_block(block_of(True, -2))
    ship(12, block_of(True, -2), at(1))
    await_block(block_of(True, 2))
    ship(13, block_of(True, 2), at(-1))
    ship(14, block_of(True, 2 * way), at(-2 * way))
    forwards = []

    def rows_of(chunk):
        return pl.ds(pl.multiple_of(chunk * LANES, LANES), LANES)

    def chunk_copy(i, chunk):
        rows = white_rt.at[rows_of(chunk)]
        return remote(rows, rows, g_fwd.at[i], g_recv.at[chunk], sibling)

    def take_jacobi(chunk):
        jac[:, rows_of(chunk)] = squares_over_epochs(white_rt[rows_of(chunk), :])

    for i in range(CHUNKS // 2):
        relay = c != (i % 2) * 8 + ((start + ASIDE[i // 2]) % 4) * 2 + k
        copy = chunk_copy(i, 2 * i + k)
        forwards.append((relay, copy))

        @pl.when(relay)
        def _():
            copy.wait_recv()
            copy.start()

    for i in range(CHUNKS // 2):
        take_jacobi(2 * i + k)
    for i in range(CHUNKS // 2):
        chunk_copy(i, 2 * i + 1 - k).wait_recv()
        take_jacobi(2 * i + 1 - k)

    leave_rt = pltpu.make_async_copy(white_rt, rt_out, out_sem.at[0])
    leave_rt.start()
    jacobi = jac[...]
    direction0 = probes[...] / jacobi / wide_row(center)
    await_bytes(ubuf.at[pl.ds(0, SIDE - 1)], u_recv.at[0])
    residual1 = probes[...] - back_product(plane_sum(ubuf[...]), white_rt[...])
    direction1 = wide_row(rho1 * rho0) * direction0 + wide_row(2.0 * rho1 / half) * (residual1 / jacobi)
    exchange_start(
        1, pack(pair_sum(jnp.dot(split(direction1), white_rt[...], preferred_element_type=F32))), last_out
    )
    keep_last = pltpu.make_async_copy(usend.at[1], last_out.at[r], out_sem.at[3])
    keep_last.start()

    for other in (False, True):
        for steps in (-3, -1, 1, 3, 4):
            await_block(block_of(other, steps))
    white_c[...] = jnp.dot(
        filt[...], cbuf[...].reshape(EPOCHS, WIDTH), preferred_element_type=F32
    ).astype(BF16)

    leave_c = pltpu.make_async_copy(white_c, c_out, out_sem.at[1])
    leave_c.start()

    state[0] = residual1
    state[1] = wide_row(2.0 * rho2 / half) / jacobi
    state[2] = direction0 + direction1 + wide_row(rho2 * rho1) * direction1
    leave_state = pltpu.make_async_copy(state, state_out, out_sem.at[2])
    leave_state.start()

    for copy in sends:
        copy.wait_send()
    for relay, copy in forwards:
        pl.when(relay)(copy.wait_send)

    @pl.when(is_owner)
    def _():
        await_bytes(rs_send.at[pl.ds(0, SIDE - 1)], rs_ssem)
        await_bytes(white_rt.at[pl.ds(0, 8 * LANES)], g_send)
        await_bytes(probes.at[:, pl.ds(0, WIDTH - LANES)], p_send)

    @pl.when(jnp.logical_not(is_owner))
    def _():
        await_bytes(probes, p_send)

    kept = jnp.logical_and(is_owner, on_diagonal)

    @pl.when(kept)
    def _():
        await_bytes(design.at[:, pl.ds(0, WIDTH - LANES)], s_send)

    @pl.when(jnp.logical_not(kept))
    def _():
        await_bytes(design, s_send)

    await_bytes(ubuf.at[pl.ds(0, SIDE - 1)], u_send.at[0])
    leave_rt.wait()
    leave_c.wait()
    leave_state.wait()

    keep_last.wait()
    await_bytes(ubuf.at[pl.ds(0, SIDE - 1)], u_send.at[1])
    await_bytes(ubuf.at[pl.ds(0, SIDE - 1)], u_recv.at[1])


def tile_kernel(
    rt_in, c_in, state_in, last_in, tile_out, answer_out,
    white_rt, white_c, state, last, answer, rows, in_sem, out_sem,
):
    load_c = pltpu.make_async_copy(c_in, white_c, in_sem.at[0])
    load_c.start()
    loads, leaves = [], []
    for part in range(STEPS):
        here = pl.ds(part * STEP, STEP)
        loads.append(pltpu.make_async_copy(rt_in.at[here], white_rt.at[here], in_sem.at[3 + part]))
        leaves.append(pltpu.make_async_copy(rows.at[part], tile_out.at[here], out_sem.at[1 + part]))
        loads[part].start()
    load_state = pltpu.make_async_copy(state_in, state, in_sem.at[1])
    load_last = pltpu.make_async_copy(last_in, last, in_sem.at[2])
    load_state.start()
    load_last.start()
    load_c.wait()
    for part in range(STEPS):
        loads[part].wait()
        rows[part] = jnp.dot(
            white_rt[part * STEP : (part + 1) * STEP], white_c[...], preferred_element_type=F32
        )
        leaves[part].start()
    load_state.wait()
    load_last.wait()
    residual2 = state[0] - back_product(plane_sum(last[...]), white_rt[...])
    answer[...] = state[2] + state[1] * residual2
    leave_answer = pltpu.make_async_copy(answer, answer_out, out_sem.at[0])
    leave_answer.start()
    for leave in leaves:
        leave.wait()
    leave_answer.wait()


def body(design, filter_taps, probes, lower_bound, upper_bound):
    smem = pl.BlockSpec(memory_space=pltpu.SMEM)
    hbm = pl.BlockSpec(memory_space=pltpu.HBM)
    dma = pltpu.SemaphoreType.DMA
    held = pl.pallas_call(
        kernel,
        out_shape=(
            jax.ShapeDtypeStruct((WIDTH, EPOCHS), BF16),
            jax.ShapeDtypeStruct((EPOCHS, WIDTH), BF16),
            jax.ShapeDtypeStruct((3, 8, WIDTH), F32),
            jax.ShapeDtypeStruct((SIDE, 16, LANES), BF16),
        ),
        in_specs=[hbm, hbm, hbm, smem, smem],
        out_specs=(hbm, hbm, hbm, hbm),
        scratch_shapes=[
            pltpu.VMEM((3, 8, WIDTH), F32),
            pltpu.VMEM((8, WIDTH), F32),
            pltpu.VMEM((BLOCK, WIDTH), BF16),
            pltpu.VMEM((1, EPOCHS), F32),
            pltpu.VMEM((8, WIDTH), F32),
            pltpu.VMEM((SIDE, BLOCK, WIDTH), BF16),
            pltpu.VMEM((SIDE, BLOCK, LANES), BF16),
            pltpu.VMEM((SIDE, 8, LANES), F32),
            pltpu.VMEM((EPOCHS, EPOCHS), BF16),
            pltpu.VMEM((EPOCHS, EPOCHS), BF16),
            pltpu.VMEM((WIDTH, EPOCHS), BF16),
            pltpu.VMEM((EPOCHS, WIDTH), BF16),
            pltpu.VMEM((2, 16, LANES), BF16),
            pltpu.VMEM((SIDE, 16, LANES), BF16),
            pltpu.VMEM((SIDE, 16, LANES), BF16),
            pltpu.VMEM((CHUNKS, 16, LANES), BF16),
            dma((3,)), dma((4,)),
            dma((15,)), dma((SIDE,)),
            dma, dma,
            dma, dma,
            dma, dma,
            dma, dma((CHUNKS // 2,)), dma((CHUNKS,)),
            dma((2,)), dma((2,)),
        ],
        compiler_params=pltpu.CompilerParams(
            collective_id=1, has_side_effects=True, vmem_limit_bytes=GRANT
        ),
        name="gather_and_solve",
    )(design, filter_taps.reshape(1, EPOCHS), probes.T, lower_bound, upper_bound)
    tile, answer = pl.pallas_call(
        tile_kernel,
        out_shape=(
            jax.ShapeDtypeStruct((WIDTH, WIDTH), F32),
            jax.ShapeDtypeStruct((8, WIDTH), F32),
        ),
        in_specs=[hbm] * 4,
        out_specs=(hbm, hbm),
        scratch_shapes=[
            pltpu.VMEM((WIDTH, EPOCHS), BF16),
            pltpu.VMEM((EPOCHS, WIDTH), BF16),
            pltpu.VMEM((3, 8, WIDTH), F32),
            pltpu.VMEM((SIDE, 16, LANES), BF16),
            pltpu.VMEM((8, WIDTH), F32),
            pltpu.VMEM((STEPS, STEP, WIDTH), F32),
            dma((3 + STEPS,)), dma((1 + STEPS,)),
        ],
        compiler_params=pltpu.CompilerParams(vmem_limit_bytes=GRANT),
        name="normal_tile",
    )(*held)
    return tile, answer.T


def solution(mesh):
    placed = (P("row", "col"), P(), P("row", "col"), P(), P())
    return jax.shard_map(
        body,
        mesh=mesh,
        in_specs=placed,
        out_specs=(P("row", "col"), P("row", "col")),
        check_vma=False,
    )
```
